256 devices in a mesh: expert: 16 (over z, x_lo), tensor: 16 (over x_hi, y, core).
Axes of the slice: x: 4 (x_hi: 2, x_lo: 2; x = x_hi * 2 + x_lo), y: 4, z: 8, core: 2. Of those that a mesh axis runs over, the one named last changes fastest.
Arguments:
- out_grad: bfloat16 [2048, 3072], P('expert', 'tensor'), may hold values from -6 to 6
- expert_ids: int32 [2048, 4], P('expert'), may hold values from 0 to 15, all different within a row; in each aligned block of 128 rows (0 to 127, 128 to 255, ...) at most 48 rows name the same one
- gate_values: float32 [2048, 4], P('expert'), may hold values from 0.05 to 1
- saved_inputs: bfloat16 [16, 768, 3072], P('expert', None, 'tensor'), may hold values from -6 to 6
- w_gate: bfloat16 [16, 3072, 5376], P('expert', None, 'tensor'), may hold values from -0.15625 to 0.15625
- w_up: bfloat16 [16, 3072, 5376], P('expert', None, 'tensor'), may hold values from -0.109375 to 0.109375
- w_down: bfloat16 [16, 5376, 3072], P('expert', 'tensor'), may hold values from -0.078125 to 0.078125
Outputs:
- in_grad: bfloat16 [2048, 3072], P('expert', 'tensor')
- grad_gate: bfloat16 [16, 3072, 5376], P('expert', None, 'tensor')
- grad_up: bfloat16 [16, 3072, 5376], P('expert', None, 'tensor')
- grad_down: bfloat16 [16, 5376, 3072], P('expert', 'tensor')
The draws below stay inside these ranges and needn't reach their ends.
Inputs may be any that keep to these rules, and one draw needn't show every extreme that they name: `expert_ids`: each row names 4 different experts. Within the 128 rows of one index of expert no expert is named more than 48 times, and in every draw some expert is named exactly 48 times within one such block.
All inputs are finite; a program needn't handle non-finite values.
Results may differ from the reference program's by a relative error of at most 0.02.
Values may be sent and summed in bfloat16 or wider, within the bound.
No kernel may reach another device: no remote copies, remote signals or barrier semaphores. Data moves between devices by JAX's collectives and lax.ppermute only.
A program may use at most 128 MiB of HBM per device.

```python
import math
import jax
import jax.numpy as jnp
import numpy as np
from jax import lax

D = 3072
FF = 5376
TOP = 4
TOK_DEV = 128
EXPERTS = 16
TOKENS = 2048
CAP = 48
SLOTS = 768
N_EXPERT = 16


def spiked(values, key, source, target, shards_of, factor):
    def block_of(dim):
        return (jnp.arange(values.shape[dim]) // (values.shape[dim] // shards_of)).reshape((-1,) + (1,) * (values.ndim - 1 - dim))

    near = jax.random.permutation(key, shards_of)[block_of(target)]
    second = (block_of(target) + shards_of // 2) % shards_of
    return jnp.where((block_of(source) == near) | (block_of(source) == second), factor * values, values)


def steps_of(key, dims, split, low, top_value):
    level = 1.0
    for position, blocks in split:
        heights = jax.random.uniform(jax.random.fold_in(jax.random.fold_in(key, 6), position), (blocks,), jnp.float32, low / len(split), top_value / len(split))
        level = level * jnp.repeat(jnp.exp(heights), dims[position] // blocks).reshape((-1,) + (1,) * (len(dims) - 1 - position))
    return level


def routed_block(own_key, own, number, rows, number_of, top, limit, skew):
    ranking = jax.random.permutation(own_key, number_of)
    crowded, common = portions_of(number_of, rows * top, limit, skew, True), portions_of(number_of, rows * top, limit, skew, False)
    places = jnp.arange(number_of)

    def named(lengths, offset_by):
        used = int((lengths > 0).sum())
        fixed = max(1, used // 4)
        shifted = fixed + (places - fixed + offset_by * (used - fixed)) % max(1, number_of - fixed)
        return jnp.zeros((number_of,), jnp.int32).at[ranking[jnp.where(places < fixed, places, shifted)]].set(jnp.asarray(lengths, jnp.int32))

    lengths = jnp.where(number % 4 == 0, named(crowded, number // 4), named(common, number - number // 4 - 1))
    mixed = jax.random.permutation(jax.random.fold_in(own, 3), number_of)
    giver, receiver = mixed[0:number_of // 2 * 2:2], mixed[1:number_of // 2 * 2:2]
    margin = jnp.minimum(lengths[giver] - 1, limit - lengths[receiver]) // 2
    margin = jnp.where((giver == ranking[0]) | (receiver == ranking[0]) | (lengths[receiver] == 0), 0, jnp.maximum(margin, 0))
    shifted = jax.random.randint(jax.random.fold_in(own, 4), (number_of // 2,), 0, 1 << 20) % (margin + 1)
    lengths = lengths.at[giver].add(-shifted).at[receiver].add(shifted)
    items = jnp.searchsorted(jnp.cumsum(lengths), jnp.arange(rows * top), side="right").astype(jnp.int32)
    table = items.reshape(top, rows).T
    table = table[jax.random.permutation(jax.random.fold_in(own, 1), rows)]
    offset_by = jax.random.randint(jax.random.fold_in(own, 2), (rows, 1), 0, top)
    return jnp.take_along_axis(table, (jnp.arange(top)[None, :] + offset_by) % top, axis=1)


def portions_of(number_of, total, limit, skew, full):
    portions = [(1 << 20) // math.isqrt(standing ** skew) + 1 for standing in range(1, number_of + 1)]
    largest = limit if full else min(limit, max(-(-total // number_of), total * portions[0] // sum(portions)))
    least = 1 if total - largest >= number_of - 1 else 0
    counts, surplus = [largest] + [least] * (number_of - 1), total - largest - least * (number_of - 1)
    while surplus > 0:
        movable = [i for i in range(1, number_of) if counts[i] < largest] or [i for i in range(1, number_of) if counts[i] < limit]
        pool, left = sum([portions[i] for i in movable]), surplus
        for i in movable:
            extra = min(limit - counts[i], max(1, left * portions[i] // pool), surplus)
            counts[i] = counts[i] + extra
            surplus = surplus - extra
    return np.array(counts)


def noise(stream_key, extent, width, bound, pieces=(), kind=jnp.bfloat16):
    values = width * jax.random.normal(stream_key, extent, jnp.float32)
    if pieces:
        values = values * steps_of(stream_key, extent, pieces, -0.22, 0.18)
    return jnp.clip(values, -bound, bound).astype(kind)


def heavy_noise(stream_key, dims, scale, bound, cuts, heavy, kind=jnp.bfloat16):
    result = scale * jax.random.normal(stream_key, dims, jnp.float32)
    if cuts:
        result = result * steps_of(stream_key, dims, cuts, -0.22, 0.18)
    return jnp.clip(spiked(result, jax.random.fold_in(stream_key, 3), *heavy), -bound, bound).astype(kind)


def setup_inputs(seed: int = 0) -> dict:
    streams_of = jax.random.split(jax.random.key(seed), 8)
    out_grad = noise(streams_of[0], (TOKENS, D), 1.0, 6.0, ((0, 16), (1, 16)))
    expert_ids_keys = jax.random.split(jax.random.fold_in(streams_of[1], 1), TOKENS // TOK_DEV)
    expert_ids_turns = jax.random.permutation(jax.random.fold_in(streams_of[1], 3), TOKENS // TOK_DEV)
    expert_ids = jax.vmap(lambda own, number: routed_block(jax.random.fold_in(streams_of[1], 2), own, number, TOK_DEV, EXPERTS, TOP, CAP, 1))(expert_ids_keys, expert_ids_turns).reshape((TOKENS, TOP))
    gate_values = jnp.clip(jnp.exp(math.log(1.0) - 2.9957323 * jax.random.uniform(streams_of[2], (TOKENS, TOP), jnp.float32) ** steps_of(streams_of[2], (TOKENS, TOP), ((0, 16),), -0.2, 0.2)), 0.05, 1.0)
    saved_inputs = noise(streams_of[3], (EXPERTS, SLOTS, D), 1.0, 6.0, ((0, 16), (2, 16)))
    w_gate = heavy_noise(streams_of[4], (EXPERTS, D, FF), D ** -0.5, 0.15625, ((0, 16), (2, 16)), (2, 1, 16, 2.0))
    w_up = noise(streams_of[5], (EXPERTS, D, FF), D ** -0.5, 0.109375, ((0, 16), (2, 16)))
    w_down = noise(streams_of[6], (EXPERTS, FF, D), FF ** -0.5, 0.078125, ((0, 16), (1, 16)))
    return dict(out_grad=out_grad, expert_ids=expert_ids, gate_values=gate_values, saved_inputs=saved_inputs, w_gate=w_gate, w_up=w_up, w_down=w_down)


def slot_index(expert_ids):
    blocks = expert_ids.reshape(N_EXPERT, TOK_DEV * TOP)
    onehot = (blocks[:, :, None] == jnp.arange(EXPERTS, dtype=jnp.int32)[None, None, :]).astype(jnp.int32)
    earlier = jnp.cumsum(onehot, axis=1) - onehot
    place = jnp.sum(earlier * onehot, axis=2).astype(jnp.int32)
    source = jnp.arange(N_EXPERT, dtype=jnp.int32)[:, None]
    return (blocks * SLOTS + source * CAP + place).reshape(-1).astype(jnp.int32)


def expert_backward(parts):
    routed, inputs, gate_mat, up_mat, down_mat = parts
    gate_pre = jnp.dot(inputs, gate_mat, preferred_element_type=jnp.float32)
    up_pre = jnp.dot(inputs, up_mat, preferred_element_type=jnp.float32)
    sigmoid_gate = jax.nn.sigmoid(gate_pre)
    activated = gate_pre * sigmoid_gate
    hidden = (activated * up_pre).astype(jnp.bfloat16)
    d_hidden = jnp.dot(routed, down_mat.T, preferred_element_type=jnp.float32)
    slope = sigmoid_gate * (1.0 + gate_pre * (1.0 - sigmoid_gate))
    d_gate = (d_hidden * up_pre * slope).astype(jnp.bfloat16)
    d_up = (d_hidden * activated).astype(jnp.bfloat16)
    grad_down = jnp.dot(hidden.T, routed, preferred_element_type=jnp.float32).astype(jnp.bfloat16)
    grad_gate = jnp.dot(inputs.T, d_gate, preferred_element_type=jnp.float32).astype(jnp.bfloat16)
    grad_up = jnp.dot(inputs.T, d_up, preferred_element_type=jnp.float32).astype(jnp.bfloat16)
    slot_grad = jnp.dot(d_gate, gate_mat.T, preferred_element_type=jnp.float32) + jnp.dot(d_up, up_mat.T, preferred_element_type=jnp.float32)
    return grad_gate, grad_up, grad_down, slot_grad


def reference(out_grad, expert_ids, gate_values, saved_inputs, w_gate, w_up, w_down):
    flat_slot = slot_index(expert_ids)
    repeated = jnp.repeat(out_grad, TOP, axis=0).astype(jnp.float32)
    scaled = (gate_values.reshape(-1)[:, None] * repeated).astype(jnp.bfloat16)
    routed = jnp.zeros((EXPERTS * SLOTS, D), jnp.bfloat16).at[flat_slot].set(scaled)
    routed = routed.reshape(EXPERTS, SLOTS, D)
    grad_gate, grad_up, grad_down, slot_grad = lax.map(expert_backward, (routed, saved_inputs, w_gate, w_up, w_down))
    picked = jnp.take(slot_grad.reshape(EXPERTS * SLOTS, D), flat_slot, axis=0)
    in_grad = jnp.sum(picked.reshape(TOKENS, TOP, D), axis=1).astype(jnp.bfloat16)
    return in_grad, grad_gate, grad_up, grad_down
```

```python
import functools

import jax
import jax.numpy as jnp
from jax import lax
from jax.experimental import pallas as pl
from jax.experimental.pallas import tpu as pltpu
from jax.sharding import PartitionSpec as P

BF16, F32 = jnp.bfloat16, jnp.float32
NT = (((1,), (1,)), ((), ()))
TN = (((0,), (0,)), ((), ()))
HERE, RIGHT, LEFT, FAR = (0, 0), (0, 1), (0, 3), (0, 2)
ACROSS, DIAG_RIGHT, DIAG_LEFT, DIAG_FAR = (1, 0), (1, 1), (1, 3), (1, 2)
VMEM_LIMIT = 56 * 1024 * 1024


def vmem(n=1):
    return [pl.BlockSpec(memory_space=pltpu.VMEM)] * n


def struct(shape, dtype):
    return jax.ShapeDtypeStruct(shape, dtype)


def call(kernel, outs, in_specs, flops, nbytes, scratch=()):
    return pl.pallas_call(
        kernel,
        out_shape=outs,
        in_specs=in_specs,
        out_specs=jax.tree.map(lambda _: pl.BlockSpec(memory_space=pltpu.VMEM), outs),
        scratch_shapes=list(scratch),
        compiler_params=pltpu.CompilerParams(vmem_limit_bytes=VMEM_LIMIT),
        cost_estimate=pl.CostEstimate(flops=flops, bytes_accessed=nbytes, transcendentals=0),
    )


def to_chip(x, dx, dy):
    pairs = [
        (((a * 4 + b) * 2 + c), (((a + dx) % 2) * 4 + (b + dy) % 4) * 2 + c)
        for a in range(2)
        for b in range(4)
        for c in range(2)
    ]
    return lax.ppermute(x, "tensor", pairs)


def to_core(x):
    return lax.ppermute(x, "tensor", [(i, i ^ 1) for i in range(16)])


def gather_pieces(x):
    rows = x.shape[0]
    h = rows // 2
    pieces = []

    def add(array, parts):
        swapped = to_core(array)
        for first, chip, at, n in parts:
            pieces.append((array, first, chip, at, n, 0))
            pieces.append((swapped, first, chip, at, n, 1))

    left, right, across = to_chip(x, 0, 1), to_chip(x, 0, 3), to_chip(x, 1, 0)
    a = to_chip(jnp.concatenate([left[:h], across[:h]]), 0, 1)
    b = to_chip(jnp.concatenate([right[h:], across[h:]]), 0, 3)
    c = to_chip(jnp.concatenate([left[h:], right[:h]]), 1, 0)
    e = to_chip(a[h:], 0, 1)
    f = to_chip(b[h:], 0, 3)
    add(x, [(0, HERE, 0, rows)])
    add(left, [(0, LEFT, 0, rows)])
    add(right, [(0, RIGHT, 0, rows)])
    add(across, [(0, ACROSS, 0, rows)])
    add(a, [(0, FAR, 0, h), (h, DIAG_LEFT, 0, h)])
    add(b, [(0, FAR, h, h), (h, DIAG_RIGHT, h, h)])
    add(c, [(0, DIAG_LEFT, h, h), (h, DIAG_RIGHT, 0, h)])
    add(e, [(0, DIAG_FAR, 0, h)])
    add(f, [(0, DIAG_FAR, h, h)])
    return pieces


def split_pieces(pieces):
    arrays, index, plan = [], {}, []
    for array, first, chip, at, n, other in pieces:
        if id(array) not in index:
            index[id(array)] = len(arrays)
            arrays.append(array)
        plan.append((index[id(array)], first, chip, at, n, other))
    return arrays, plan


def chip_of(where, rel):
    return ((where[0] + rel[0]) % 2) * 4 + (where[1] + rel[1]) % 4


def assemble(plan, refs, full, where, sems):
    share = full.shape[0] // 16
    copies = []
    for i, (number, first, chip, at, n, other) in enumerate(plan):
        core = where[2] if other == 0 else 1 - where[2]
        row = pl.multiple_of((chip_of(where, chip) * 2 + core) * share + at, 16)
        copies.append(
            pltpu.make_async_copy(
                refs[number].at[pl.ds(first, n)], full.at[pl.ds(row, n)], sems.at[i]
            )
        )
    for copy in copies:
        copy.start()
    for copy in copies:
        copy.wait()


def route_kernel(ids_ref, gates_ref, grad_ref, routed_ref, pick_ref):
    top, tokens = ids_ref.shape
    slots = routed_ref.shape[0]
    groups = 16
    capacity = slots // groups
    expert = lax.broadcasted_iota(jnp.int32, (groups, tokens), 0)
    named = jnp.zeros((groups, tokens), F32)
    gate = jnp.zeros((groups, tokens), F32)
    for k in range(top):
        hit = expert == ids_ref[k : k + 1, :]
        named = named + jnp.where(hit, 1.0, 0.0)
        gate = gate + jnp.where(hit, gates_ref[k : k + 1, :], 0.0)
    earlier = lax.broadcasted_iota(jnp.int32, (tokens, tokens), 0) < lax.broadcasted_iota(
        jnp.int32, (tokens, tokens), 1
    )
    place = jnp.dot(
        named.astype(BF16),
        jnp.where(earlier, 1.0, 0.0).astype(BF16),
        preferred_element_type=F32,
    ).astype(jnp.int32)
    place = jnp.where(named > 0.5, place, -1)
    at = lax.broadcasted_iota(jnp.int32, (capacity, tokens), 0)
    for e in range(groups):
        hit = at == place[e : e + 1, :]
        one = jnp.where(hit, 1.0, 0.0).astype(BF16)
        scale = jnp.sum(jnp.where(hit, gate[e : e + 1, :], 0.0), axis=1, keepdims=True)
        rows = slice(e * capacity, (e + 1) * capacity)
        pick_ref[rows, :] = one
        picked = lax.dot_general(one, grad_ref[...], NT, preferred_element_type=F32)
        routed_ref[rows, :] = (picked * scale).astype(BF16)


def combine_kernel(back_ref, pick_ref, out_ref):
    out_ref[...] = lax.dot_general(
        back_ref[...], pick_ref[...], TN, preferred_element_type=F32
    ).astype(BF16)


def forward_kernel(plan, n, where, *refs):
    pieces, (gate_ref, up_ref), (full, act_ref, slope_ref, hidden_ref, sems) = (
        refs[:n],
        refs[n : n + 2],
        refs[n + 2 :],
    )
    assemble(plan, pieces, full, where, sems)
    width = 256
    for j in range(full.shape[1] // width):
        cols = slice(j * width, (j + 1) * width)
        x = full[:, cols]
        gate = jnp.dot(gate_ref[...], x, preferred_element_type=F32)
        up = jnp.dot(up_ref[...], x, preferred_element_type=F32)
        sig = jax.nn.sigmoid(gate)
        act = gate * sig
        act_ref[:, cols] = act
        slope_ref[:, cols] = up * (sig * (1.0 + gate * (1.0 - sig)))
        hidden_ref[:, cols] = (act * up).astype(BF16)


def slot_blocks(rels, where, gate_ref, up_ref, d_gate, d_up, own_ref, other_ref):
    share = own_ref.shape[1]
    first_core = where[2] == 0
    for i, rel in enumerate(rels):
        cols = pl.ds(pl.multiple_of(chip_of(where, rel) * 2 * share, 128), 2 * share)
        block = lax.dot_general(
            gate_ref[:, cols], d_gate, TN, preferred_element_type=F32
        ) + lax.dot_general(up_ref[:, cols], d_up, TN, preferred_element_type=F32)
        low, high = block[:share].astype(BF16), block[share:].astype(BF16)
        own_ref[i] = jnp.where(first_core, low, high)
        other_ref[i] = jnp.where(first_core, high, low)


def backward_kernel(plan, n, rels, where, *refs):
    pieces = refs[:n]
    down_ref, gate_ref, up_ref, act_ref, slope_ref = refs[n : n + 5]
    full, d_gate_ref, d_up_ref, own_ref, other_ref, sems = refs[n + 5 :]
    assemble(plan, pieces, full, where, sems)
    width = 256
    for j in range(full.shape[1] // width):
        cols = slice(j * width, (j + 1) * width)
        d_hidden = jnp.dot(down_ref[...], full[:, cols], preferred_element_type=F32)
        d_gate_ref[:, cols] = (d_hidden * slope_ref[:, cols]).astype(BF16)
        d_up_ref[:, cols] = (d_hidden * act_ref[:, cols]).astype(BF16)
    slot_blocks(
        rels, where, gate_ref, up_ref, d_gate_ref[...], d_up_ref[...], own_ref, other_ref
    )


def slot_kernel(rels, where, gate_ref, up_ref, d_gate_ref, d_up_ref, own_ref, other_ref):
    slot_blocks(
        rels, where, gate_ref, up_ref, d_gate_ref[...], d_up_ref[...], own_ref, other_ref
    )


def weight_kernel(rows_ref, full_ref, out_ref):
    width = 512
    for j in range(full_ref.shape[0] // width):
        cols = slice(j * width, (j + 1) * width)
        out_ref[:, cols] = lax.dot_general(
            rows_ref[...], full_ref[cols, :], NT, preferred_element_type=F32
        ).astype(BF16)


def plus(*terms):
    total = terms[0].astype(F32)
    for term in terms[1:]:
        total = total + term.astype(F32)
    return total.astype(BF16)


def shards(out_grad, expert_ids, gate_values, saved_inputs, w_gate, w_up, w_down):
    tokens, share = out_grad.shape
    slots = saved_inputs.shape[1]
    units = w_gate.shape[2]
    width = w_gate.shape[1]
    me = lax.axis_index("tensor")
    where = jnp.stack([me // 8, (me // 2) % 4, me % 2]).astype(jnp.int32)
    smem = [pl.BlockSpec(memory_space=pltpu.SMEM)]
    anywhere = pl.BlockSpec(memory_space=pl.ANY)
    gate_t, up_t, down = w_gate[0].T, w_up[0].T, w_down[0]
    one_matmul = 2 * slots * units * width

    routed, pick = call(
        route_kernel,
        (struct((slots, share), BF16), struct((slots, tokens), BF16)),
        vmem(3),
        2 * slots * tokens * share,
        10**6,
    )(expert_ids.T, gate_values.T, out_grad.T)
    pieces, plan = split_pieces(gather_pieces(saved_inputs[0].T))
    routed = lax.all_to_all(routed, "expert", split_axis=0, concat_axis=0, tiled=True)
    routed_pieces, routed_plan = split_pieces(gather_pieces(routed.T))

    n = len(pieces)
    inputs, act, slope, hidden = call(
        functools.partial(forward_kernel, plan, n),
        (
            struct((width, slots), BF16),
            struct((units, slots), F32),
            struct((units, slots), F32),
            struct((units, slots), BF16),
        ),
        smem + [anywhere] * n + vmem(2),
        2 * one_matmul,
        10**7,
        [pltpu.SemaphoreType.DMA((len(plan),))],
    )(where, *pieces, gate_t, up_t)

    def pair(count):
        return (struct((count, share, slots), BF16), struct((count, share, slots), BF16))

    n = len(routed_pieces)
    rels = [DIAG_FAR], [DIAG_RIGHT, DIAG_LEFT, FAR], [HERE, RIGHT, LEFT, ACROSS]
    full, d_gate, d_up, own_a, other_a = call(
        functools.partial(backward_kernel, routed_plan, n, rels[0]),
        (
            struct((width, slots), BF16),
            struct((units, slots), BF16),
            struct((units, slots), BF16),
        )
        + pair(1),
        smem + [anywhere] * n + vmem(5),
        one_matmul,
        10**7,
        [pltpu.SemaphoreType.DMA((len(routed_plan),))],
    )(where, *routed_pieces, down, gate_t, up_t, act, slope)
    own_b, other_b = call(
        functools.partial(slot_kernel, rels[1]), pair(3), smem + vmem(4), one_matmul, 10**7
    )(where, gate_t, up_t, d_gate, d_up)
    own_c, other_c = call(
        functools.partial(slot_kernel, rels[2]), pair(4), smem + vmem(4), one_matmul, 10**7
    )(where, gate_t, up_t, d_gate, d_up)
    other_a, other_b, other_c = to_core(other_a), to_core(other_b), to_core(other_c)

    h = share // 2
    far = plus(own_a[0], other_a[0])
    to_left, to_right = to_chip(far[:h], 0, 3), to_chip(far[h:], 0, 1)
    diag_right = jnp.concatenate(
        [plus(own_b[0, :h], other_b[0, :h]), plus(own_b[0, h:], other_b[0, h:], to_right)]
    )
    diag_left = jnp.concatenate(
        [plus(own_b[1, :h], other_b[1, :h], to_left), plus(own_b[1, h:], other_b[1, h:])]
    )
    far = plus(own_b[2], other_b[2])
    a = to_chip(jnp.concatenate([far[:h], diag_left[:h]]), 0, 3)
    b = to_chip(jnp.concatenate([far[h:], diag_right[h:]]), 0, 1)
    c = to_chip(jnp.concatenate([diag_left[h:], diag_right[:h]]), 1, 0)
    right = jnp.concatenate(
        [plus(own_c[1, :h], other_c[1, :h], c[h:]), plus(own_c[1, h:], other_c[1, h:], b[:h])]
    )
    left = jnp.concatenate(
        [plus(own_c[2, :h], other_c[2, :h], a[:h]), plus(own_c[2, h:], other_c[2, h:], c[:h])]
    )
    across = jnp.concatenate(
        [plus(own_c[3, :h], other_c[3, :h], a[h:]), plus(own_c[3, h:], other_c[3, h:], b[h:])]
    )
    summed = plus(
        own_c[0], other_c[0], to_chip(right, 0, 1), to_chip(left, 0, 3), to_chip(across, 1, 0)
    )
    back = lax.all_to_all(summed.T, "expert", split_axis=0, concat_axis=0, tiled=True)
    in_grad = call(
        combine_kernel, struct((share, tokens), BF16), vmem(2), 2 * slots * tokens * share, 10**6
    )(back, pick)

    def weight_grad(rows, columns):
        return call(
            weight_kernel, struct((units, width), BF16), vmem(2), one_matmul, 10**7
        )(rows, columns)

    grad_down = weight_grad(hidden, full)
    grad_gate = weight_grad(d_gate, inputs)
    grad_up = weight_grad(d_up, inputs)
    return in_grad.T, grad_gate.T[None], grad_up.T[None], grad_down[None]


def solution(mesh):
    return jax.shard_map(
        shards,
        mesh=mesh,
        in_specs=(
            P("expert", "tensor"),
            P("expert", None),
            P("expert", None),
            P("expert", None, "tensor"),
            P("expert", None, "tensor"),
            P("expert", None, "tensor"),
            P("expert", "tensor", None),
        ),
        out_specs=(
            P("expert", "tensor"),
            P("expert", None, "tensor"),
            P("expert", None, "tensor"),
            P("expert", "tensor", None),
        ),
        check_vma=False,
    )
```

```python
import functools

import jax
import jax.numpy as jnp
from jax import lax
from jax.experimental import pallas as pl
from jax.experimental.pallas import tpu as pltpu
from jax.sharding import PartitionSpec as P

BF16, F32 = jnp.bfloat16, jnp.float32
NT = (((1,), (1,)), ((), ()))
TN = (((0,), (0,)), ((), ()))
HERE, RIGHT, LEFT, FAR = (0, 0), (0, 1), (0, 3), (0, 2)
ACROSS, DIAG_RIGHT, DIAG_LEFT, DIAG_FAR = (1, 0), (1, 1), (1, 3), (1, 2)
MB = 1024 * 1024


def vmem(n=1):
    return [pl.BlockSpec(memory_space=pltpu.VMEM)] * n


def anywhere(n=1):
    return [pl.BlockSpec(memory_space=pl.ANY)] * n


def struct(shape, dtype):
    return jax.ShapeDtypeStruct(shape, dtype)


def call(kernel, outs, in_specs, out_specs, flops, limit, scratch=()):
    return pl.pallas_call(
        kernel,
        out_shape=tuple(outs),
        in_specs=in_specs,
        out_specs=tuple(out_specs),
        scratch_shapes=list(scratch),
        compiler_params=pltpu.CompilerParams(vmem_limit_bytes=limit * MB),
        cost_estimate=pl.CostEstimate(flops=flops, bytes_accessed=10**7, transcendentals=0),
    )


def after(x, *earlier):
    return lax.optimization_barrier((x,) + earlier)[0]


def to_chip(x, dx, dy):
    pairs = [
        (((a * 4 + b) * 2 + c), (((a + dx) % 2) * 4 + (b + dy) % 4) * 2 + c)
        for a in range(2)
        for b in range(4)
        for c in range(2)
    ]
    return lax.ppermute(x, "tensor", pairs)


def to_core(x):
    return lax.ppermute(x, "tensor", [(i, i ^ 1) for i in range(16)])


def pack_kernel(plan, n, *refs):
    for out, parts in zip(refs[n:], plan):
        row = 0
        for number, first, rows, turned in parts:
            value = refs[number][first : first + rows, :]
            value = value.T if turned else value
            out[row : row + value.shape[0], :] = value
            row += value.shape[0]


def pack(*outs):
    arrays, index, plan, shapes = [], {}, [], []
    for parts in outs:
        steps, total, columns = [], 0, 0
        for array, *rows in parts:
            if id(array) not in index:
                index[id(array)] = len(arrays)
                arrays.append(array)
            first, count = rows or (0, array.shape[0])
            steps.append((index[id(array)], first, count, not rows))
            total += count if rows else array.shape[1]
            columns = array.shape[1] if rows else count
        plan.append(steps)
        shapes.append(struct((total, columns), BF16))
    made = call(
        functools.partial(pack_kernel, plan, len(arrays)),
        shapes,
        vmem(len(arrays)),
        vmem(len(shapes)),
        10**6,
        12,
    )(*arrays)
    return made if len(made) > 1 else made[0]


def first_step(x):
    return to_chip(x, 0, 1), to_chip(x, 0, 3), to_chip(x, 1, 0)


def second_step(left, right, across, to_right=(), to_left=()):
    h = across.shape[0] // 2
    steps = pack(
        [(left, 0, h), (across, 0, h), *to_right],
        [(right, h, h), (across, h, h), *to_left],
        [(left, h, h), (right, 0, h)],
    )
    return steps, (to_chip(steps[0], 0, 1), to_chip(steps[1], 0, 3), to_chip(steps[2], 1, 0))


def most(x, left, right, across, a, b, c):
    rows = x.shape[0]
    own = pack([(array, 0, rows) for array in (x, left, right, across, a, b, c)])
    return own, to_core(own)


def pieces_plan(rows):
    h = rows // 2
    plan = []
    for other in range(2):
        for i, chip in enumerate((HERE, LEFT, RIGHT, ACROSS)):
            plan.append((other, i * rows, chip, 0, rows, other))
        for i, (chip, at) in enumerate(
            (
                (FAR, 0),
                (DIAG_LEFT, 0),
                (FAR, h),
                (DIAG_RIGHT, h),
                (DIAG_LEFT, h),
                (DIAG_RIGHT, 0),
            )
        ):
            plan.append((other, 4 * rows + i * h, chip, at, h, other))
        plan.append((2 + other, 0, DIAG_FAR, 0, h, other))
        plan.append((4 + other, 0, DIAG_FAR, h, h, other))
    return plan


def chip_of(where, rel):
    return ((where[0] + rel[0]) % 2) * 4 + (where[1] + rel[1]) % 4


def assemble(plan, refs, full, where):
    share = full.shape[0] // 16
    for number, first, chip, at, n, other in plan:
        core = where[2] if other == 0 else 1 - where[2]
        row = pl.multiple_of((chip_of(where, chip) * 2 + core) * share + at, 32)
        full[pl.ds(row, n), :] = refs[number][first : first + n, :]


def start_assemble(plan, refs, full, where, sems):
    share = full.shape[0] // 16
    copies = []
    for i, (number, first, chip, at, n, other) in enumerate(plan):
        core = where[2] if other == 0 else 1 - where[2]
        row = pl.multiple_of((chip_of(where, chip) * 2 + core) * share + at, 32)
        copies.append(
            pltpu.make_async_copy(
                refs[number].at[pl.ds(first, n)], full.at[pl.ds(row, n)], sems.at[i]
            )
        )
    for copy in copies:
        copy.start()
    return copies


def fetch(pairs, sems, first=0):
    copies = [
        pltpu.make_async_copy(source, target, sems.at[first + i])
        for i, (source, target) in enumerate(pairs)
    ]
    for copy in copies:
        copy.start()
    return copies


def wait(copies):
    for copy in copies:
        copy.wait()


def route_kernel(ids_ref, gates_ref, grad_ref, routed_ref, pick_ref):
    top, tokens = ids_ref.shape
    slots = routed_ref.shape[0]
    groups = 16
    capacity = slots // groups
    expert = lax.broadcasted_iota(jnp.int32, (groups, tokens), 0)
    named = jnp.zeros((groups, tokens), F32)
    gate = jnp.zeros((groups, tokens), F32)
    for k in range(top):
        hit = expert == ids_ref[k : k + 1, :]
        named = named + jnp.where(hit, 1.0, 0.0)
        gate = gate + jnp.where(hit, gates_ref[k : k + 1, :], 0.0)
    earlier = lax.broadcasted_iota(jnp.int32, (tokens, tokens), 0) < lax.broadcasted_iota(
        jnp.int32, (tokens, tokens), 1
    )
    place = jnp.dot(
        named.astype(BF16),
        jnp.where(earlier, 1.0, 0.0).astype(BF16),
        preferred_element_type=F32,
    ).astype(jnp.int32)
    place = jnp.where(named > 0.5, place, -1)
    at = lax.broadcasted_iota(jnp.int32, (capacity, tokens), 0)
    for e in range(groups):
        hit = at == place[e : e + 1, :]
        one = jnp.where(hit, 1.0, 0.0).astype(BF16)
        scale = jnp.sum(jnp.where(hit, gate[e : e + 1, :], 0.0), axis=1, keepdims=True)
        rows = slice(e * capacity, (e + 1) * capacity)
        pick_ref[rows, :] = one
        picked = lax.dot_general(one, grad_ref[...], NT, preferred_element_type=F32)
        routed_ref[rows, :] = (picked * scale).astype(BF16)


def sum_kernel(*refs):
    total = refs[0][...].astype(F32)
    for ref in refs[1:-1]:
        total = total + ref[...].astype(F32)
    refs[-1][...] = total.T.astype(BF16)


def combine_kernel(back_ref, pick_ref, out_ref):
    out_ref[...] = lax.dot_general(
        back_ref[...], pick_ref[...], TN, preferred_element_type=F32
    ).astype(BF16)


def forward_kernel(plan, n, where, *refs):
    pieces, (gate_ref, up_ref) = refs[:n], refs[n : n + 2]
    act_ref, slope_ref, hidden_ref, full = refs[n + 2 :]
    assemble(plan, pieces, full, where)
    width = 256
    for j in range(full.shape[1] // width):
        cols = slice(j * width, (j + 1) * width)
        x = full[:, cols]
        gate = jnp.dot(gate_ref[...], x, preferred_element_type=F32)
        up = jnp.dot(up_ref[...], x, preferred_element_type=F32)
        sig = jax.nn.sigmoid(gate)
        act = gate * sig
        act_ref[:, cols] = act
        slope_ref[:, cols] = up * (sig * (1.0 + gate * (1.0 - sig)))
        hidden_ref[:, cols] = (act * up).astype(BF16)


def slot_blocks(rels, where, gate_ref, up_ref, d_gate, d_up, own_ref, other_ref):
    share = own_ref.shape[1]
    first_core = where[2] == 0
    for i, rel in enumerate(rels):
        cols = pl.ds(pl.multiple_of(chip_of(where, rel) * 2 * share, 128), 2 * share)
        block = lax.dot_general(
            gate_ref[:, cols], d_gate, TN, preferred_element_type=F32
        ) + lax.dot_general(up_ref[:, cols], d_up, TN, preferred_element_type=F32)
        low, high = block[:share].astype(BF16), block[share:].astype(BF16)
        own_ref[i] = jnp.where(first_core, low, high)
        other_ref[i] = jnp.where(first_core, high, low)


def backward_kernel(plan, n, rels, where, *refs):
    pieces = refs[:n]
    down_ref, gate_ref, up_ref, act_ref, slope_ref = refs[n : n + 5]
    d_gate_ref, d_up_ref, own_ref, other_ref, full = refs[n + 5 :]
    assemble(plan, pieces, full, where)
    width = 256
    for j in range(full.shape[1] // width):
        cols = slice(j * width, (j + 1) * width)
        d_hidden = jnp.dot(down_ref[...], full[:, cols], preferred_element_type=F32)
        d_gate_ref[:, cols] = (d_hidden * slope_ref[:, cols]).astype(BF16)
        d_up_ref[:, cols] = (d_hidden * act_ref[:, cols]).astype(BF16)
    slot_blocks(
        rels, where, gate_ref, up_ref, d_gate_ref[...], d_up_ref[...], own_ref, other_ref
    )


def slot_kernel(rels, where, gate_ref, up_ref, d_gate_ref, d_up_ref, own_ref, other_ref):
    slot_blocks(
        rels, where, gate_ref, up_ref, d_gate_ref[...], d_up_ref[...], own_ref, other_ref
    )


def weight_kernel(plan, n, where, *refs):
    inputs, routed = refs[:n], refs[n : 2 * n]
    hidden_ref, d_gate_ref, d_up_ref = refs[2 * n : 2 * n + 3]
    outs = refs[2 * n + 3 : 2 * n + 6]
    full, full_routed, *kept, sems, rsems, osems = refs[2 * n + 6 :]
    parts = start_assemble(plan, inputs, full, where, sems)
    routed_parts = start_assemble(plan, routed, full_routed, where, rsems)
    width = 512
    wait(parts)
    sent = []
    for k, (rows_ref, source) in enumerate(
        ((d_gate_ref, full), (d_up_ref, full), (hidden_ref, full_routed))
    ):
        if k == 2:
            wait(routed_parts)
        for j in range(source.shape[0] // width):
            cols = slice(j * width, (j + 1) * width)
            kept[k][:, cols] = lax.dot_general(
                rows_ref[...], source[cols, :], NT, preferred_element_type=F32
            ).astype(BF16)
        sent += fetch([(kept[k], outs[k])], osems, k)
    wait(sent)


def plus(*terms):
    total = terms[0].astype(F32)
    for term in terms[1:]:
        total = total + term.astype(F32)
    return total.astype(BF16)


def shards(out_grad, expert_ids, gate_values, saved_inputs, w_gate, w_up, w_down):
    tokens, share = out_grad.shape
    slots = saved_inputs.shape[1]
    units = w_gate.shape[2]
    width = w_gate.shape[1]
    wide = 2 * share
    me = lax.axis_index("tensor")
    where = jnp.stack([me // 8, (me // 2) % 4, me % 2]).astype(jnp.int32)
    smem = [pl.BlockSpec(memory_space=pltpu.SMEM)]
    dma = pltpu.SemaphoreType.DMA
    gate_t, up_t, down = w_gate[0].T, w_up[0].T, w_down[0]
    one_matmul = 2 * slots * units * width

    routed, pick = call(
        route_kernel,
        (struct((slots, share), BF16), struct((slots, tokens), BF16)),
        vmem(3),
        vmem(2),
        2 * slots * tokens * share,
        60,
    )(expert_ids.T, gate_values.T, out_grad.T)
    h = share // 2
    plan = pieces_plan(share)
    n = 6
    x = saved_inputs[0].T
    left, right, across = first_step(x)
    steps, (a, b, c) = second_step(left, right, across)
    routed = lax.all_to_all(routed, "expert", split_axis=0, concat_axis=0, tiled=True)
    own, other = most(x, left, right, across, a, b, c)
    r = pack([(after(routed, *steps),)])
    left, right, across = first_step(r)
    _, (a, b, c) = second_step(left, right, across, [(a, h, h)], [(b, h, h)])
    e, f = a[share:], b[share:]
    input_pieces = (own, other, e, to_core(e), f, to_core(f))
    e, f = pack([(a, h, h)], [(b, h, h)])
    ready = e
    e, f = to_chip(e, 0, 1), to_chip(f, 0, 3)
    act, slope, hidden = call(
        functools.partial(forward_kernel, plan, n),
        (
            struct((units, slots), F32),
            struct((units, slots), F32),
            struct((units, slots), BF16),
        ),
        smem + vmem(n + 2),
        vmem(3),
        2 * one_matmul,
        24,
        [pltpu.VMEM((width, slots), BF16)],
    )(after(where, ready), *input_pieces, gate_t, up_t)
    e, f = lax.optimization_barrier((e, f, act))[:2]
    own, other = most(r, left, right, across, a, b, c)
    routed_pieces = (own, other, e, to_core(e), f, to_core(f))

    def pair(count):
        return [struct((count, share, slots), BF16)] * 2

    rels = [DIAG_FAR], [DIAG_RIGHT, DIAG_LEFT, FAR], [HERE, RIGHT, LEFT, ACROSS]
    d_gate, d_up, own_a, other_a = call(
        functools.partial(backward_kernel, plan, n, rels[0]),
        [struct((units, slots), BF16)] * 2 + pair(1),
        smem + vmem(n + 5),
        vmem(4),
        one_matmul,
        24,
        [pltpu.VMEM((width, slots), BF16)],
    )(where, *routed_pieces, down, gate_t, up_t, act, slope)

    def slot_call(k, where):
        return call(
            functools.partial(slot_kernel, rels[k]),
            pair(len(rels[k])),
            smem + vmem(4),
            vmem(2),
            one_matmul,
            16,
        )(where, gate_t, up_t, d_gate, d_up)

    other_a = to_core(other_a)
    own_b, other_b = slot_call(1, where)
    far = plus(after(own_a[0], other_b), other_a[0])
    to_left, to_right = to_chip(far[:h], 0, 3), to_chip(far[h:], 0, 1)
    other_b = to_core(after(other_b, far))
    own_c, other_c = slot_call(2, after(where, far, other_b))
    diag_right = jnp.concatenate(
        [plus(own_b[0, :h], other_b[0, :h]), plus(own_b[0, h:], other_b[0, h:], to_right)]
    )
    diag_left = jnp.concatenate(
        [plus(own_b[1, :h], other_b[1, :h], to_left), plus(own_b[1, h:], other_b[1, h:])]
    )
    far = plus(own_b[2], other_b[2])
    steps = lax.optimization_barrier(
        (
            jnp.concatenate([far[:h], diag_left[:h]]),
            jnp.concatenate([far[h:], diag_right[h:]]),
            jnp.concatenate([diag_left[h:], diag_right[:h]]),
            own_c,
        )
    )
    other_c = to_core(other_c)
    a, b, c = to_chip(steps[0], 0, 3), to_chip(steps[1], 0, 1), to_chip(steps[2], 1, 0)
    right = jnp.concatenate(
        [plus(own_c[1, :h], other_c[1, :h], c[h:]), plus(own_c[1, h:], other_c[1, h:], b[:h])]
    )
    left = jnp.concatenate(
        [plus(own_c[2, :h], other_c[2, :h], a[:h]), plus(own_c[2, h:], other_c[2, h:], c[:h])]
    )
    across = jnp.concatenate(
        [plus(own_c[3, :h], other_c[3, :h], a[h:]), plus(own_c[3, h:], other_c[3, h:], b[h:])]
    )
    grad_gate, grad_up, grad_down = call(
        functools.partial(weight_kernel, plan, n),
        [struct((units, width), BF16)] * 3,
        smem + anywhere(2 * n) + vmem(3),
        anywhere(3),
        3 * one_matmul,
        60,
        [pltpu.VMEM((width, slots), BF16)] * 2
        + [pltpu.VMEM((units, width), BF16)] * 3
        + [dma((len(plan),)), dma((len(plan),)), dma((3,))],
    )(after(where, left, right, across), *input_pieces, *routed_pieces, hidden, d_gate, d_up)
    (summed,) = call(
        sum_kernel, [struct((slots, share), BF16)], vmem(5), vmem(1), 10**6, 8
    )(own_c[0], other_c[0], to_chip(right, 0, 1), to_chip(left, 0, 3), to_chip(across, 1, 0))
    back = lax.all_to_all(summed, "expert", split_axis=0, concat_axis=0, tiled=True)
    (in_grad,) = call(
        combine_kernel,
        [struct((share, tokens), BF16)],
        vmem(2),
        vmem(1),
        2 * slots * tokens * share,
        8,
    )(back, pick)
    return in_grad.T, grad_gate.T[None], grad_up.T[None], grad_down[None]


def solution(mesh):
    return jax.shard_map(
        shards,
        mesh=mesh,
        in_specs=(
            P("expert", "tensor"),
            P("expert", None),
            P("expert", None),
            P("expert", None, "tensor"),
            P("expert", None, "tensor"),
            P("expert", None, "tensor"),
            P("expert", "tensor", None),
        ),
        out_specs=(
            P("expert", "tensor"),
            P("expert", None, "tensor"),
            P("expert", None, "tensor"),
            P("expert", "tensor", None),
        ),
        check_vma=False,
    )
```

```python
import functools

import jax
import jax.numpy as jnp
from jax import lax
from jax.experimental import pallas as pl
from jax.experimental.pallas import tpu as pltpu
from jax.sharding import PartitionSpec as P

BF16, F32 = jnp.bfloat16, jnp.float32
NT = (((1,), (1,)), ((), ()))
TN = (((0,), (0,)), ((), ()))
HERE, RIGHT, LEFT, FAR = (0, 0), (0, 1), (0, 3), (0, 2)
ACROSS, DIAG_RIGHT, DIAG_LEFT, DIAG_FAR = (1, 0), (1, 1), (1, 3), (1, 2)
MB = 1024 * 1024


def vmem(n=1):
    return [pl.BlockSpec(memory_space=pltpu.VMEM)] * n


def anywhere(n=1):
    return [pl.BlockSpec(memory_space=pl.ANY)] * n


def struct(shape, dtype):
    return jax.ShapeDtypeStruct(shape, dtype)


def call(kernel, outs, in_specs, out_specs, flops, limit, scratch=()):
    return pl.pallas_call(
        kernel,
        out_shape=tuple(outs),
        in_specs=in_specs,
        out_specs=tuple(out_specs),
        scratch_shapes=list(scratch),
        compiler_params=pltpu.CompilerParams(vmem_limit_bytes=limit * MB),
        cost_estimate=pl.CostEstimate(flops=flops, bytes_accessed=10**7, transcendentals=0),
    )


def after(x, *earlier):
    return lax.optimization_barrier((x,) + earlier)[0]


def to_chip(x, dx, dy):
    pairs = [
        (((a * 4 + b) * 2 + c), (((a + dx) % 2) * 4 + (b + dy) % 4) * 2 + c)
        for a in range(2)
        for b in range(4)
        for c in range(2)
    ]
    return lax.ppermute(x, "tensor", pairs)


def to_core(x):
    return lax.ppermute(x, "tensor", [(i, i ^ 1) for i in range(16)])


def pack_kernel(plan, n, *refs):
    for out, parts in zip(refs[n:], plan):
        row = 0
        for number, first, rows, turned in parts:
            value = refs[number][first : first + rows, :]
            value = value.T if turned else value
            out[row : row + value.shape[0], :] = value
            row += value.shape[0]


def pack(*outs, flops=10**6):
    arrays, index, plan, shapes = [], {}, [], []
    for parts in outs:
        steps, total, columns = [], 0, 0
        for array, *rows in parts:
            if id(array) not in index:
                index[id(array)] = len(arrays)
                arrays.append(array)
            first, count = rows or (0, array.shape[0])
            steps.append((index[id(array)], first, count, not rows))
            total += count if rows else array.shape[1]
            columns = array.shape[1] if rows else count
        plan.append(steps)
        shapes.append(struct((total, columns), BF16))
    made = call(
        functools.partial(pack_kernel, plan, len(arrays)),
        shapes,
        vmem(len(arrays)),
        vmem(len(shapes)),
        flops,
        12,
    )(*arrays)
    return made if len(made) > 1 else made[0]


def first_step(x):
    across, left, right = to_chip(x, 1, 0), to_chip(x, 0, 1), to_chip(x, 0, 3)
    return left, right, across


def second_step(left, right, across, to_right=(), to_left=(), flops=10**6):
    h = across.shape[0] // 2
    steps = pack(
        [(left, 0, h), (across, 0, h), *to_right],
        [(right, h, h), (across, h, h), *to_left],
        [(left, h, h), (right, 0, h)],
        flops=flops,
    )
    c, a, b = to_chip(steps[2], 1, 0), to_chip(steps[0], 0, 1), to_chip(steps[1], 0, 3)
    return steps, (a, b, c)


def most(x, left, right, across, a, b, c):
    rows = x.shape[0]
    own = pack([(array, 0, rows) for array in (x, left, right, across, a, b, c)])
    return own, to_core(own)


def most_plan(rows):
    h = rows // 2
    plan = []
    for other in range(2):
        for i, chip in enumerate((HERE, LEFT, RIGHT, ACROSS)):
            plan.append((other, i * rows, chip, 0, rows, other))
        for i, (chip, at) in enumerate(
            (
                (FAR, 0),
                (DIAG_LEFT, 0),
                (FAR, h),
                (DIAG_RIGHT, h),
                (DIAG_LEFT, h),
                (DIAG_RIGHT, 0),
            )
        ):
            plan.append((other, 4 * rows + i * h, chip, at, h, other))
    return plan


def last_plan(rows, joined):
    if joined:
        return [(other, 0, DIAG_FAR, 0, rows, other) for other in range(2)]
    h = rows // 2
    return [(2 * i + other, 0, DIAG_FAR, i * h, h, other) for i in range(2) for other in range(2)]


def shifted(plan, by):
    return [(number + by, *rest) for number, *rest in plan]


def chip_of(where, rel):
    return ((where[0] + rel[0]) % 2) * 4 + (where[1] + rel[1]) % 4


def assemble(plan, refs, full, where):
    share = full.shape[0] // 16
    for number, first, chip, at, n, other in plan:
        core = where[2] if other == 0 else 1 - where[2]
        row = pl.multiple_of((chip_of(where, chip) * 2 + core) * share + at, 32)
        full[pl.ds(row, n), :] = refs[number][first : first + n, :]


def clear(chip, full, where):
    wide = full.shape[0] // 8
    row = pl.multiple_of(chip_of(where, chip) * wide, 32)
    full[pl.ds(row, wide), :] = jnp.zeros((wide, full.shape[1]), full.dtype)


def far_rows(joined, refs, block, where):
    share = block.shape[0] // 2
    for number, first, chip, at, n, other in last_plan(share, joined):
        core = where[2] if other == 0 else 1 - where[2]
        row = pl.multiple_of(core * share + at, 32)
        block[pl.ds(row, n), :] = refs[number][first : first + n, :]
    return pl.ds(pl.multiple_of(chip_of(where, DIAG_FAR) * 2 * share, 128), 2 * share)


def start_assemble(plan, refs, full, where, sems):
    share = full.shape[0] // 16
    copies = []
    for i, (number, first, chip, at, n, other) in enumerate(plan):
        core = where[2] if other == 0 else 1 - where[2]
        row = pl.multiple_of((chip_of(where, chip) * 2 + core) * share + at, 32)
        copies.append(
            pltpu.make_async_copy(
                refs[number].at[pl.ds(first, n)], full.at[pl.ds(row, n)], sems.at[i]
            )
        )
    for copy in copies:
        copy.start()
    return copies


def fetch(pairs, sems, first=0):
    copies = [
        pltpu.make_async_copy(source, target, sems.at[first + i])
        for i, (source, target) in enumerate(pairs)
    ]
    for copy in copies:
        copy.start()
    return copies


def wait(copies):
    for copy in copies:
        copy.wait()


def route_kernel(ids_ref, gates_ref, grad_ref, routed_ref, pick_ref):
    top, tokens = ids_ref.shape
    slots = routed_ref.shape[0]
    groups = 16
    capacity = slots // groups
    expert = lax.broadcasted_iota(jnp.int32, (groups, tokens), 0)
    named = jnp.zeros((groups, tokens), F32)
    gate = jnp.zeros((groups, tokens), F32)
    for k in range(top):
        hit = expert == ids_ref[k : k + 1, :]
        named = named + jnp.where(hit, 1.0, 0.0)
        gate = gate + jnp.where(hit, gates_ref[k : k + 1, :], 0.0)
    earlier = lax.broadcasted_iota(jnp.int32, (tokens, tokens), 0) < lax.broadcasted_iota(
        jnp.int32, (tokens, tokens), 1
    )
    place = jnp.dot(
        named.astype(BF16),
        jnp.where(earlier, 1.0, 0.0).astype(BF16),
        preferred_element_type=F32,
    ).astype(jnp.int32)
    place = jnp.where(named > 0.5, place, -1)
    at = lax.broadcasted_iota(jnp.int32, (capacity, tokens), 0)
    for e in range(groups):
        hit = at == place[e : e + 1, :]
        one = jnp.where(hit, 1.0, 0.0).astype(BF16)
        scale = jnp.sum(jnp.where(hit, gate[e : e + 1, :], 0.0), axis=1, keepdims=True)
        rows = slice(e * capacity, (e + 1) * capacity)
        pick_ref[rows, :] = one
        picked = lax.dot_general(one, grad_ref[...], NT, preferred_element_type=F32)
        routed_ref[rows, :] = (picked * scale).astype(BF16)


def sum_kernel(*refs):
    total = refs[0][...].astype(F32)
    for ref in refs[1:-1]:
        total = total + ref[...].astype(F32)
    refs[-1][...] = total.T.astype(BF16)


def combine_kernel(back_ref, pick_ref, out_ref):
    out_ref[...] = lax.dot_general(
        back_ref[...], pick_ref[...], TN, preferred_element_type=F32
    ).astype(BF16)


def most_kernel(plan, where, own_ref, other_ref, *refs):
    n = (len(refs) - 1) // 2
    weights, outs, full = refs[:n], refs[n : 2 * n], refs[2 * n]
    clear(DIAG_FAR, full, where)
    assemble(plan, (own_ref, other_ref), full, where)
    for weight_ref, out_ref in zip(weights, outs):
        out_ref[...] = jnp.dot(weight_ref[...], full[...], preferred_element_type=F32)


def forward_kernel(where, own_ref, other_ref, gate_ref, up_ref, gate_most, up_most, *refs):
    act_ref, slope_ref, hidden_ref, block = refs
    far = far_rows(True, (own_ref, other_ref), block, where)
    width = 256
    for j in range(block.shape[1] // width):
        cols = slice(j * width, (j + 1) * width)
        x = block[:, cols]
        gate = gate_most[:, cols] + jnp.dot(gate_ref[:, far], x, preferred_element_type=F32)
        up = up_most[:, cols] + jnp.dot(up_ref[:, far], x, preferred_element_type=F32)
        sig = jax.nn.sigmoid(gate)
        act = gate * sig
        act_ref[:, cols] = act
        slope_ref[:, cols] = up * (sig * (1.0 + gate * (1.0 - sig)))
        hidden_ref[:, cols] = (act * up).astype(BF16)


def slot_blocks(rels, where, gate_ref, up_ref, d_gate, d_up, own_ref, other_ref):
    share = own_ref.shape[1]
    first_core = where[2] == 0
    for i, rel in enumerate(rels):
        cols = pl.ds(pl.multiple_of(chip_of(where, rel) * 2 * share, 128), 2 * share)
        block = lax.dot_general(
            gate_ref[:, cols], d_gate, TN, preferred_element_type=F32
        ) + lax.dot_general(up_ref[:, cols], d_up, TN, preferred_element_type=F32)
        low, high = block[:share].astype(BF16), block[share:].astype(BF16)
        own_ref[i] = jnp.where(first_core, low, high)
        other_ref[i] = jnp.where(first_core, high, low)


def backward_kernel(rels, where, *refs):
    pieces = refs[:4]
    down_ref, gate_ref, up_ref, act_ref, slope_ref, most_ref = refs[4:10]
    d_gate_ref, d_up_ref, own_ref, other_ref, block = refs[10:]
    far = far_rows(False, pieces, block, where)
    width = 256
    for j in range(block.shape[1] // width):
        cols = slice(j * width, (j + 1) * width)
        d_hidden = most_ref[:, cols] + jnp.dot(
            down_ref[:, far], block[:, cols], preferred_element_type=F32
        )
        d_gate_ref[:, cols] = (d_hidden * slope_ref[:, cols]).astype(BF16)
        d_up_ref[:, cols] = (d_hidden * act_ref[:, cols]).astype(BF16)
    slot_blocks(
        rels, where, gate_ref, up_ref, d_gate_ref[...], d_up_ref[...], own_ref, other_ref
    )


def slot_kernel(rels, where, gate_ref, up_ref, d_gate_ref, d_up_ref, own_ref, other_ref):
    slot_blocks(
        rels, where, gate_ref, up_ref, d_gate_ref[...], d_up_ref[...], own_ref, other_ref
    )


def weight_kernel(plans, where, *refs):
    inputs, routed = refs[:4], refs[4:10]
    hidden_ref, d_gate_ref, d_up_ref = refs[10:13]
    outs = refs[13:16]
    full, full_routed, *kept, sems, rsems, osems = refs[16:]
    parts = start_assemble(plans[0], inputs, full, where, sems)
    routed_parts = start_assemble(plans[1], routed, full_routed, where, rsems)
    width = 512
    wait(parts)
    sent = []
    for k, (rows_ref, source) in enumerate(
        ((d_gate_ref, full), (d_up_ref, full), (hidden_ref, full_routed))
    ):
        if k == 2:
            wait(routed_parts)
        for j in range(source.shape[0] // width):
            cols = slice(j * width, (j + 1) * width)
            kept[k][:, cols] = lax.dot_general(
                rows_ref[...], source[cols, :], NT, preferred_element_type=F32
            ).astype(BF16)
        sent += fetch([(kept[k], outs[k])], osems, k)
    wait(sent)


def plus(*terms):
    total = terms[0].astype(F32)
    for term in terms[1:]:
        total = total + term.astype(F32)
    return total.astype(BF16)


def shards(out_grad, expert_ids, gate_values, saved_inputs, w_gate, w_up, w_down):
    tokens, share = out_grad.shape
    slots = saved_inputs.shape[1]
    units = w_gate.shape[2]
    width = w_gate.shape[1]
    wide = 2 * share
    me = lax.axis_index("tensor")
    where = jnp.stack([me // 8, (me // 2) % 4, me % 2]).astype(jnp.int32)
    smem = [pl.BlockSpec(memory_space=pltpu.SMEM)]
    dma = pltpu.SemaphoreType.DMA
    gate_t, up_t, down = w_gate[0].T, w_up[0].T, w_down[0]
    one_matmul = 2 * slots * units * width

    routed, pick = call(
        route_kernel,
        (struct((slots, share), BF16), struct((slots, tokens), BF16)),
        vmem(3),
        vmem(2),
        2 * slots * tokens * share,
        60,
    )(expert_ids.T, gate_values.T, out_grad.T)
    h = share // 2
    plan = most_plan(share)
    plans = [plan + shifted(last_plan(share, joined), 2) for joined in (True, False)]
    x = saved_inputs[0].T
    left, right, across = first_step(x)
    steps, (a, b, c) = second_step(left, right, across)
    routed = lax.all_to_all(routed, "expert", split_axis=0, concat_axis=0, tiled=True)
    own, other = most(x, left, right, across, a, b, c)
    r = pack([(after(routed, *steps),)])
    left, right, across = first_step(r)
    steps, (a, b, c) = second_step(
        left, right, across, [(a, h, h)], [(b, h, h)], 20000000000
    )

    def most_call(weights, where, own, other):
        n = len(weights)
        return call(
            functools.partial(most_kernel, plan),
            [struct((units, slots), F32)] * n,
            smem + vmem(n + 2),
            vmem(n),
            n * one_matmul,
            24,
            [pltpu.VMEM((width, slots), BF16)],
        )(where, own, other, *weights)

    gate_most, up_most = most_call((gate_t, up_t), after(where, *steps), own, other)
    a, b, c = lax.optimization_barrier((a, b, c, gate_most))[:3]
    e, f, last = pack([(a, h, h)], [(b, h, h)], [(a, share, h), (b, share, h)])
    input_pieces = (own, other, last, to_core(last))
    act, slope, hidden = call(
        forward_kernel,
        (
            struct((units, slots), F32),
            struct((units, slots), F32),
            struct((units, slots), BF16),
        ),
        smem + vmem(6),
        vmem(3),
        one_matmul,
        24,
        [pltpu.VMEM((wide, slots), BF16)],
    )(after(where, e), *input_pieces[2:], gate_t, up_t, gate_most, up_most)
    e, f = to_chip(e, 0, 1), to_chip(f, 0, 3)
    e, f = lax.optimization_barrier((e, f, act))[:2]
    own, other = most(r, left, right, across, a, b, c)
    (d_hidden_most,) = most_call((down,), where, own, other)
    routed_pieces = (own, other, e, to_core(e), f, to_core(f))

    def pair(count):
        return [struct((count, share, slots), BF16)] * 2

    rels = [DIAG_FAR], [DIAG_RIGHT, DIAG_LEFT, FAR], [HERE, RIGHT, LEFT, ACROSS]
    d_gate, d_up, own_a, other_a = call(
        functools.partial(backward_kernel, rels[0]),
        [struct((units, slots), BF16)] * 2 + pair(1),
        smem + vmem(10),
        vmem(4),
        one_matmul,
        24,
        [pltpu.VMEM((wide, slots), BF16)],
    )(where, *routed_pieces[2:], down, gate_t, up_t, act, slope, d_hidden_most)

    def slot_call(k, where):
        return call(
            functools.partial(slot_kernel, rels[k]),
            pair(len(rels[k])),
            smem + vmem(4),
            vmem(2),
            one_matmul,
            16,
        )(where, gate_t, up_t, d_gate, d_up)

    other_a = to_core(other_a)
    own_b, other_b = slot_call(1, where)
    far = plus(after(own_a[0], other_b), other_a[0])
    to_left, to_right = to_chip(far[:h], 0, 3), to_chip(far[h:], 0, 1)
    other_b = to_core(after(other_b, far))
    own_c, other_c = slot_call(2, after(where, far, other_b))
    diag_right = jnp.concatenate(
        [plus(own_b[0, :h], other_b[0, :h]), plus(own_b[0, h:], other_b[0, h:], to_right)]
    )
    diag_left = jnp.concatenate(
        [plus(own_b[1, :h], other_b[1, :h], to_left), plus(own_b[1, h:], other_b[1, h:])]
    )
    far = plus(own_b[2], other_b[2])
    steps = lax.optimization_barrier(
        (
            jnp.concatenate([far[:h], diag_left[:h]]),
            jnp.concatenate([far[h:], diag_right[h:]]),
            jnp.concatenate([diag_left[h:], diag_right[:h]]),
            own_c,
        )
    )
    other_c = to_core(other_c)
    c, a, b = to_chip(steps[2], 1, 0), to_chip(steps[0], 0, 3), to_chip(steps[1], 0, 1)
    right = jnp.concatenate(
        [plus(own_c[1, :h], other_c[1, :h], c[h:]), plus(own_c[1, h:], other_c[1, h:], b[:h])]
    )
    left = jnp.concatenate(
        [plus(own_c[2, :h], other_c[2, :h], a[:h]), plus(own_c[2, h:], other_c[2, h:], c[:h])]
    )
    across = jnp.concatenate(
        [plus(own_c[3, :h], other_c[3, :h], a[h:]), plus(own_c[3, h:], other_c[3, h:], b[h:])]
    )
    grad_gate, grad_up, grad_down = call(
        functools.partial(weight_kernel, plans),
        [struct((units, width), BF16)] * 3,
        smem + anywhere(10) + vmem(3),
        anywhere(3),
        3 * one_matmul,
        60,
        [pltpu.VMEM((width, slots), BF16)] * 2
        + [pltpu.VMEM((units, width), BF16)] * 3
        + [dma((len(plans[0]),)), dma((len(plans[1]),)), dma((3,))],
    )(after(where, left, right, across), *input_pieces, *routed_pieces, hidden, d_gate, d_up)
    across, right, left = to_chip(across, 1, 0), to_chip(right, 0, 1), to_chip(left, 0, 3)
    (summed,) = call(
        sum_kernel, [struct((slots, share), BF16)], vmem(5), vmem(1), 10**6, 8
    )(own_c[0], other_c[0], across, right, left)
    back = lax.all_to_all(summed, "expert", split_axis=0, concat_axis=0, tiled=True)
    (in_grad,) = call(
        combine_kernel,
        [struct((share, tokens), BF16)],
        vmem(2),
        vmem(1),
        2 * slots * tokens * share,
        8,
    )(back, pick)
    return in_grad.T, grad_gate.T[None], grad_up.T[None], grad_down[None]


def solution(mesh):
    return jax.shard_map(
        shards,
        mesh=mesh,
        in_specs=(
            P("expert", "tensor"),
            P("expert", None),
            P("expert", None),
            P("expert", None, "tensor"),
            P("expert", None, "tensor"),
            P("expert", None, "tensor"),
            P("expert", "tensor", None),
        ),
        out_specs=(
            P("expert", "tensor"),
            P("expert", None, "tensor"),
            P("expert", None, "tensor"),
            P("expert", "tensor", None),
        ),
        check_vma=False,
    )
```

```python
import functools

import jax
import jax.numpy as jnp
from jax import lax
from jax.experimental import pallas as pl
from jax.experimental.pallas import tpu as pltpu
from jax.sharding import PartitionSpec as P

BF16, F32 = jnp.bfloat16, jnp.float32
NT = (((1,), (1,)), ((), ()))
TN = (((0,), (0,)), ((), ()))
HERE, RIGHT, LEFT, FAR = (0, 0), (0, 1), (0, 3), (0, 2)
ACROSS, DIAG_RIGHT, DIAG_LEFT, DIAG_FAR = (1, 0), (1, 1), (1, 3), (1, 2)
MB = 1024 * 1024


def vmem(n=1):
    return [pl.BlockSpec(memory_space=pltpu.VMEM)] * n


def anywhere(n=1):
    return [pl.BlockSpec(memory_space=pl.ANY)] * n


def struct(shape, dtype):
    return jax.ShapeDtypeStruct(shape, dtype)


def call(kernel, outs, in_specs, out_specs, flops, limit, scratch=()):
    return pl.pallas_call(
        kernel,
        out_shape=tuple(outs),
        in_specs=in_specs,
        out_specs=tuple(out_specs),
        scratch_shapes=list(scratch),
        compiler_params=pltpu.CompilerParams(vmem_limit_bytes=limit * MB),
        cost_estimate=pl.CostEstimate(flops=flops, bytes_accessed=10**7, transcendentals=0),
    )


def after(x, *earlier):
    return lax.optimization_barrier((x,) + earlier)[0]


def to_chip(x, dx, dy):
    pairs = [
        (((a * 4 + b) * 2 + c), (((a + dx) % 2) * 4 + (b + dy) % 4) * 2 + c)
        for a in range(2)
        for b in range(4)
        for c in range(2)
    ]
    return lax.ppermute(x, "tensor", pairs)


def to_core(x):
    return lax.ppermute(x, "tensor", [(i, i ^ 1) for i in range(16)])


def pack_kernel(plan, n, *refs):
    for out, parts in zip(refs[n:], plan):
        row = 0
        for number, first, rows, turned in parts:
            value = refs[number][first : first + rows, :]
            value = value.T if turned else value
            out[row : row + value.shape[0], :] = value
            row += value.shape[0]


def pack(*outs, flops=10**6):
    arrays, index, plan, shapes = [], {}, [], []
    for parts in outs:
        steps, total, columns = [], 0, 0
        for array, *rows in parts:
            if id(array) not in index:
                index[id(array)] = len(arrays)
                arrays.append(array)
            first, count = rows or (0, array.shape[0])
            steps.append((index[id(array)], first, count, not rows))
            total += count if rows else array.shape[1]
            columns = array.shape[1] if rows else count
        plan.append(steps)
        shapes.append(struct((total, columns), BF16))
    made = call(
        functools.partial(pack_kernel, plan, len(arrays)),
        shapes,
        vmem(len(arrays)),
        vmem(len(shapes)),
        flops,
        12,
    )(*arrays)
    return made if len(made) > 1 else made[0]


def first_step(x):
    across, left, right = to_chip(x, 1, 0), to_chip(x, 0, 1), to_chip(x, 0, 3)
    return left, right, across


def second_step(left, right, across, to_right=(), to_left=(), flops=10**6):
    h = across.shape[0] // 2
    steps = pack(
        [(left, 0, h), (across, 0, h), *to_right],
        [(right, h, h), (across, h, h), *to_left],
        [(left, h, h), (right, 0, h)],
        flops=flops,
    )
    c, a, b = to_chip(steps[2], 1, 0), to_chip(steps[0], 0, 1), to_chip(steps[1], 0, 3)
    return steps, (a, b, c)


def most(x, left, right, across, a, b, c):
    rows = x.shape[0]
    own = pack([(array, 0, rows) for array in (x, left, right, across, a, b, c)])
    return own, to_core(own)


def most_plan(rows):
    h = rows // 2
    plan = []
    for other in range(2):
        for i, chip in enumerate((HERE, LEFT, RIGHT, ACROSS)):
            plan.append((other, i * rows, chip, 0, rows, other))
        for i, (chip, at) in enumerate(
            (
                (FAR, 0),
                (DIAG_LEFT, 0),
                (FAR, h),
                (DIAG_RIGHT, h),
                (DIAG_LEFT, h),
                (DIAG_RIGHT, 0),
            )
        ):
            plan.append((other, 4 * rows + i * h, chip, at, h, other))
    return plan


def last_plan(rows, joined):
    if joined:
        return [(other, 0, DIAG_FAR, 0, rows, other) for other in range(2)]
    h = rows // 2
    return [(2 * i + other, 0, DIAG_FAR, i * h, h, other) for i in range(2) for other in range(2)]


def shifted(plan, by):
    return [(number + by, *rest) for number, *rest in plan]


def chip_of(where, rel):
    return ((where[0] + rel[0]) % 2) * 4 + (where[1] + rel[1]) % 4


def assemble(plan, refs, full, where):
    share = full.shape[0] // 16
    for number, first, chip, at, n, other in plan:
        core = where[2] if other == 0 else 1 - where[2]
        row = pl.multiple_of((chip_of(where, chip) * 2 + core) * share + at, 32)
        full[pl.ds(row, n), :] = refs[number][first : first + n, :]


def clear(chip, full, where):
    wide = full.shape[0] // 8
    row = pl.multiple_of(chip_of(where, chip) * wide, 32)
    full[pl.ds(row, wide), :] = jnp.zeros((wide, full.shape[1]), full.dtype)


def far_rows(joined, refs, block, where):
    share = block.shape[0] // 2
    for number, first, chip, at, n, other in last_plan(share, joined):
        core = where[2] if other == 0 else 1 - where[2]
        row = pl.multiple_of(core * share + at, 32)
        block[pl.ds(row, n), :] = refs[number][first : first + n, :]
    return pl.ds(pl.multiple_of(chip_of(where, DIAG_FAR) * 2 * share, 128), 2 * share)


def start_assemble(plan, refs, full, where, sems):
    share = full.shape[0] // 16
    copies = []
    for i, (number, first, chip, at, n, other) in enumerate(plan):
        core = where[2] if other == 0 else 1 - where[2]
        row = pl.multiple_of((chip_of(where, chip) * 2 + core) * share + at, 32)
        copies.append(
            pltpu.make_async_copy(
                refs[number].at[pl.ds(first, n)], full.at[pl.ds(row, n)], sems.at[i]
            )
        )
    for copy in copies:
        copy.start()
    return copies


def fetch(pairs, sems, first=0):
    copies = [
        pltpu.make_async_copy(source, target, sems.at[first + i])
        for i, (source, target) in enumerate(pairs)
    ]
    for copy in copies:
        copy.start()
    return copies


def wait(copies):
    for copy in copies:
        copy.wait()


def route_kernel(ids_ref, gates_ref, grad_ref, routed_ref, pick_ref):
    top, tokens = ids_ref.shape
    slots = pick_ref.shape[0]
    groups = 16
    capacity = slots // groups
    expert = lax.broadcasted_iota(jnp.int32, (groups, tokens), 0)
    named = jnp.zeros((groups, tokens), F32)
    gate = jnp.zeros((groups, tokens), F32)
    for k in range(top):
        hit = expert == ids_ref[k : k + 1, :]
        named = named + jnp.where(hit, 1.0, 0.0)
        gate = gate + jnp.where(hit, gates_ref[k : k + 1, :], 0.0)
    earlier = lax.broadcasted_iota(jnp.int32, (tokens, tokens), 0) < lax.broadcasted_iota(
        jnp.int32, (tokens, tokens), 1
    )
    place = jnp.dot(
        named.astype(BF16),
        jnp.where(earlier, 1.0, 0.0).astype(BF16),
        preferred_element_type=F32,
    ).astype(jnp.int32)
    place = jnp.where(named > 0.5, place, -1)
    at = lax.broadcasted_iota(jnp.int32, (capacity, tokens), 0)
    half = capacity // 2
    for pair in range(0, groups, 2):
        rows, low, high = [], [], []
        for e in (pair, pair + 1):
            hit = at == place[e : e + 1, :]
            one = jnp.where(hit, 1.0, 0.0)
            scale = jnp.sum(jnp.where(hit, gate[e : e + 1, :], 0.0), axis=1, keepdims=True)
            picked = lax.dot_general(
                one.astype(BF16), grad_ref[...], NT, preferred_element_type=F32
            )
            rows.append(side_by_side(picked * scale, half))
            low.append(one[:half])
            high.append(one[half:])
        place_of = slice(pair * half, (pair + 2) * half)
        routed_ref[place_of, :] = jnp.concatenate(rows).astype(BF16)
        pick_ref[place_of, :] = jnp.concatenate(low).astype(BF16)
        pick_ref[groups * half + pair * half : groups * half + (pair + 2) * half, :] = (
            jnp.concatenate(high).astype(BF16)
        )


def side_by_side(rows, half):
    return jnp.concatenate([rows[:half], rows[half:]], axis=1)


def apart_kernel(routed_ref, out_ref):
    count, wide = routed_ref.shape
    share, capacity = wide // 2, 2 * count // 16
    rows = routed_ref[...].astype(F32).reshape(16, capacity // 2, wide)
    rows = jnp.concatenate([rows[:, :, :share], rows[:, :, share:]], axis=1)
    out_ref[...] = rows.reshape(2 * count, share).T.astype(BF16)


def sum_kernel(*refs):
    total = refs[0][...].astype(F32)
    for ref in refs[1:-1]:
        total = total + ref[...].astype(F32)
    share, slots = total.shape
    half = slots // 32
    rows = total.T.reshape(16, 2 * half, share)
    rows = jnp.concatenate([rows[:, :half], rows[:, half:]], axis=2)
    refs[-1][...] = rows.reshape(16 * half, 2 * share).astype(BF16)


def merge_kernel(own_ref, other_ref, c_ref, b_ref, a_ref, right_ref, left_ref, across_ref):
    h = c_ref.shape[0] // 2
    low, high = slice(0, h), slice(h, 2 * h)
    for out_ref, i, rows, part_ref, part in (
        (right_ref, 1, low, c_ref, high),
        (right_ref, 1, high, b_ref, low),
        (left_ref, 2, low, a_ref, low),
        (left_ref, 2, high, c_ref, low),
        (across_ref, 3, low, a_ref, high),
        (across_ref, 3, high, b_ref, high),
    ):
        total = own_ref[i, rows, :].astype(F32) + other_ref[i, rows, :].astype(F32)
        out_ref[rows, :] = (total + part_ref[part, :].astype(F32)).astype(BF16)


def combine_kernel(back_ref, pick_ref, out_ref):
    count, share = back_ref.shape[0], out_ref.shape[0]
    first = lax.dot_general(
        back_ref[...], pick_ref[:count, :], TN, preferred_element_type=F32
    )
    second = lax.dot_general(
        back_ref[...], pick_ref[count:, :], TN, preferred_element_type=F32
    )
    out_ref[...] = (first[:share] + second[share:]).astype(BF16)


def most_kernel(plan, where, own_ref, other_ref, *refs):
    n = (len(refs) - 1) // 2
    weights, outs, full = refs[:n], refs[n : 2 * n], refs[2 * n]
    clear(DIAG_FAR, full, where)
    assemble(plan, (own_ref, other_ref), full, where)
    for weight_ref, out_ref in zip(weights, outs):
        out_ref[...] = jnp.dot(weight_ref[...], full[...], preferred_element_type=F32)


def forward_kernel(where, own_ref, other_ref, gate_ref, up_ref, gate_most, up_most, *refs):
    act_ref, slope_ref, hidden_ref, block = refs
    far = far_rows(True, (own_ref, other_ref), block, where)
    width = 256
    for j in range(block.shape[1] // width):
        cols = slice(j * width, (j + 1) * width)
        x = block[:, cols]
        gate = gate_most[:, cols] + jnp.dot(gate_ref[:, far], x, preferred_element_type=F32)
        up = up_most[:, cols] + jnp.dot(up_ref[:, far], x, preferred_element_type=F32)
        sig = jax.nn.sigmoid(gate)
        act = gate * sig
        act_ref[:, cols] = act
        slope_ref[:, cols] = up * (sig * (1.0 + gate * (1.0 - sig)))
        hidden_ref[:, cols] = (act * up).astype(BF16)


def slot_blocks(rels, where, gate_ref, up_ref, d_gate, d_up, own_ref, other_ref):
    share = own_ref.shape[1]
    first_core = where[2] == 0
    for i, rel in enumerate(rels):
        cols = pl.ds(pl.multiple_of(chip_of(where, rel) * 2 * share, 128), 2 * share)
        block = lax.dot_general(
            gate_ref[:, cols], d_gate, TN, preferred_element_type=F32
        ) + lax.dot_general(up_ref[:, cols], d_up, TN, preferred_element_type=F32)
        low, high = block[:share].astype(BF16), block[share:].astype(BF16)
        own_ref[i] = jnp.where(first_core, low, high)
        other_ref[i] = jnp.where(first_core, high, low)


def backward_kernel(rels, where, *refs):
    pieces = refs[:4]
    down_ref, gate_ref, up_ref, act_ref, slope_ref, most_ref = refs[4:10]
    d_gate_ref, d_up_ref, own_ref, other_ref, block = refs[10:]
    far = far_rows(False, pieces, block, where)
    width = 256
    for j in range(block.shape[1] // width):
        cols = slice(j * width, (j + 1) * width)
        d_hidden = most_ref[:, cols] + jnp.dot(
            down_ref[:, far], block[:, cols], preferred_element_type=F32
        )
        d_gate_ref[:, cols] = (d_hidden * slope_ref[:, cols]).astype(BF16)
        d_up_ref[:, cols] = (d_hidden * act_ref[:, cols]).astype(BF16)
    slot_blocks(
        rels, where, gate_ref, up_ref, d_gate_ref[...], d_up_ref[...], own_ref, other_ref
    )


def slot_kernel(rels, where, gate_ref, up_ref, d_gate_ref, d_up_ref, own_ref, other_ref):
    slot_blocks(
        rels, where, gate_ref, up_ref, d_gate_ref[...], d_up_ref[...], own_ref, other_ref
    )


def weight_kernel(plans, where, *refs):
    inputs, routed = refs[:4], refs[4:10]
    hidden_ref, d_gate_ref, d_up_ref = refs[10:13]
    outs = refs[13:16]
    full, full_routed, *kept, sems, rsems, osems = refs[16:]
    parts = start_assemble(plans[0], inputs, full, where, sems)
    routed_parts = start_assemble(plans[1], routed, full_routed, where, rsems)
    width = 512
    wait(parts)
    sent = []
    for k, (rows_ref, source) in enumerate(
        ((d_gate_ref, full), (d_up_ref, full), (hidden_ref, full_routed))
    ):
        if k == 2:
            wait(routed_parts)
        for j in range(source.shape[0] // width):
            cols = slice(j * width, (j + 1) * width)
            kept[k][:, cols] = lax.dot_general(
                rows_ref[...], source[cols, :], NT, preferred_element_type=F32
            ).astype(BF16)
        sent += fetch([(kept[k], outs[k])], osems, k)
    wait(sent)


def plus(*terms):
    total = terms[0].astype(F32)
    for term in terms[1:]:
        total = total + term.astype(F32)
    return total.astype(BF16)


def shards(out_grad, expert_ids, gate_values, saved_inputs, w_gate, w_up, w_down):
    tokens, share = out_grad.shape
    slots = saved_inputs.shape[1]
    units = w_gate.shape[2]
    width = w_gate.shape[1]
    wide = 2 * share
    me = lax.axis_index("tensor")
    where = jnp.stack([me // 8, (me // 2) % 4, me % 2]).astype(jnp.int32)
    smem = [pl.BlockSpec(memory_space=pltpu.SMEM)]
    dma = pltpu.SemaphoreType.DMA
    gate_t, up_t, down = w_gate[0].T, w_up[0].T, w_down[0]
    one_matmul = 2 * slots * units * width

    routed, pick = call(
        route_kernel,
        (struct((slots // 2, wide), BF16), struct((slots, tokens), BF16)),
        vmem(3),
        vmem(2),
        2 * slots * tokens * share,
        60,
    )(expert_ids.T, gate_values.T, out_grad.T)
    h = share // 2
    plan = most_plan(share)
    plans = [plan + shifted(last_plan(share, joined), 2) for joined in (True, False)]
    x = saved_inputs[0].T
    left, right, across = first_step(x)
    steps, (a, b, c) = second_step(left, right, across)
    routed = lax.all_to_all(routed, "expert", split_axis=0, concat_axis=0, tiled=True)
    own, other = most(x, left, right, across, a, b, c)
    (r,) = call(
        apart_kernel, [struct((share, slots), BF16)], vmem(1), vmem(1), 10**6, 8
    )(after(routed, *steps))
    left, right, across = first_step(r)
    steps, (a, b, c) = second_step(
        left, right, across, [(a, h, h)], [(b, h, h)], 20000000000
    )

    def most_call(weights, where, own, other):
        n = len(weights)
        return call(
            functools.partial(most_kernel, plan),
            [struct((units, slots), F32)] * n,
            smem + vmem(n + 2),
            vmem(n),
            n * one_matmul,
            24,
            [pltpu.VMEM((width, slots), BF16)],
        )(where, own, other, *weights)

    gate_most, up_most = most_call((gate_t, up_t), after(where, *steps), own, other)
    a, b, c = lax.optimization_barrier((a, b, c, gate_most))[:3]
    e, f, last = pack([(a, h, h)], [(b, h, h)], [(a, share, h), (b, share, h)])
    input_pieces = (own, other, last, to_core(last))
    act, slope, hidden = call(
        forward_kernel,
        (
            struct((units, slots), F32),
            struct((units, slots), F32),
            struct((units, slots), BF16),
        ),
        smem + vmem(6),
        vmem(3),
        one_matmul,
        24,
        [pltpu.VMEM((wide, slots), BF16)],
    )(after(where, e), *input_pieces[2:], gate_t, up_t, gate_most, up_most)
    e, f = to_chip(e, 0, 1), to_chip(f, 0, 3)
    e, f = lax.optimization_barrier((e, f, act))[:2]
    own, other = most(r, left, right, across, a, b, c)
    (d_hidden_most,) = most_call((down,), where, own, other)
    routed_pieces = (own, other, e, to_core(e), f, to_core(f))

    def pair(count):
        return [struct((count, share, slots), BF16)] * 2

    rels = [DIAG_FAR], [DIAG_RIGHT, DIAG_LEFT, FAR], [HERE, RIGHT, LEFT, ACROSS]
    d_gate, d_up, own_a, other_a = call(
        functools.partial(backward_kernel, rels[0]),
        [struct((units, slots), BF16)] * 2 + pair(1),
        smem + vmem(10),
        vmem(4),
        one_matmul,
        24,
        [pltpu.VMEM((wide, slots), BF16)],
    )(where, *routed_pieces[2:], down, gate_t, up_t, act, slope, d_hidden_most)

    def slot_call(k, where):
        return call(
            functools.partial(slot_kernel, rels[k]),
            pair(len(rels[k])),
            smem + vmem(4),
            vmem(2),
            one_matmul,
            16,
        )(where, gate_t, up_t, d_gate, d_up)

    other_a = to_core(other_a)
    own_b, other_b = slot_call(1, where)
    far = plus(after(own_a[0], other_b), other_a[0])
    to_left, to_right = to_chip(far[:h], 0, 3), to_chip(far[h:], 0, 1)
    other_b = to_core(after(other_b, far))
    own_c, other_c = slot_call(2, after(where, far, other_b))
    diag_right = jnp.concatenate(
        [plus(own_b[0, :h], other_b[0, :h]), plus(own_b[0, h:], other_b[0, h:], to_right)]
    )
    diag_left = jnp.concatenate(
        [plus(own_b[1, :h], other_b[1, :h], to_left), plus(own_b[1, h:], other_b[1, h:])]
    )
    far = plus(own_b[2], other_b[2])
    steps = lax.optimization_barrier(
        (
            jnp.concatenate([far[:h], diag_left[:h]]),
            jnp.concatenate([far[h:], diag_right[h:]]),
            jnp.concatenate([diag_left[h:], diag_right[:h]]),
            own_c,
        )
    )
    other_c = to_core(other_c)
    c, b, a = to_chip(steps[2], 1, 0), to_chip(steps[1], 0, 1), to_chip(steps[0], 0, 3)
    right, left, across = call(
        merge_kernel,
        [struct((share, slots), BF16)] * 3,
        vmem(5),
        vmem(3),
        10**6,
        16,
    )(own_c, other_c, c, b, a)
    grad_gate, grad_up, grad_down = call(
        functools.partial(weight_kernel, plans),
        [struct((units, width), BF16)] * 3,
        smem + anywhere(10) + vmem(3),
        anywhere(3),
        3 * one_matmul,
        60,
        [pltpu.VMEM((width, slots), BF16)] * 2
        + [pltpu.VMEM((units, width), BF16)] * 3
        + [dma((len(plans[0]),)), dma((len(plans[1]),)), dma((3,))],
    )(after(where, left, right, across), *input_pieces, *routed_pieces, hidden, d_gate, d_up)
    across, right, left = to_chip(across, 1, 0), to_chip(right, 0, 1), to_chip(left, 0, 3)
    (summed,) = call(
        sum_kernel, [struct((slots // 2, wide), BF16)], vmem(5), vmem(1), 10**6, 8
    )(own_c[0], other_c[0], across, right, left)
    back = lax.all_to_all(summed, "expert", split_axis=0, concat_axis=0, tiled=True)
    (in_grad,) = call(
        combine_kernel,
        [struct((share, tokens), BF16)],
        vmem(2),
        vmem(1),
        2 * slots * tokens * share,
        8,
    )(back, pick)
    return in_grad.T, grad_gate.T[None], grad_up.T[None], grad_down[None]


def solution(mesh):
    return jax.shard_map(
        shards,
        mesh=mesh,
        in_specs=(
            P("expert", "tensor"),
            P("expert", None),
            P("expert", None),
            P("expert", None, "tensor"),
            P("expert", None, "tensor"),
            P("expert", None, "tensor"),
            P("expert", "tensor", None),
        ),
        out_specs=(
            P("expert", "tensor"),
            P("expert", None, "tensor"),
            P("expert", None, "tensor"),
            P("expert", "tensor", None),
        ),
        check_vma=False,
    )
```

```python
import functools

import jax
import jax.numpy as jnp
from jax import lax
from jax.experimental import pallas as pl
from jax.experimental.pallas import tpu as pltpu
from jax.sharding import PartitionSpec as P

BF16, F32 = jnp.bfloat16, jnp.float32
NT = (((1,), (1,)), ((), ()))
TN = (((0,), (0,)), ((), ()))
HERE, RIGHT, LEFT, FAR = (0, 0), (0, 1), (0, 3), (0, 2)
ACROSS, DIAG_RIGHT, DIAG_LEFT, DIAG_FAR = (1, 0), (1, 1), (1, 3), (1, 2)
MB = 1024 * 1024


def vmem(n=1):
    return [pl.BlockSpec(memory_space=pltpu.VMEM)] * n


def anywhere(n=1):
    return [pl.BlockSpec(memory_space=pl.ANY)] * n


def struct(shape, dtype):
    return jax.ShapeDtypeStruct(shape, dtype)


def call(kernel, outs, in_specs, out_specs, flops, limit, scratch=()):
    return pl.pallas_call(
        kernel,
        out_shape=tuple(outs),
        in_specs=in_specs,
        out_specs=tuple(out_specs),
        scratch_shapes=list(scratch),
        compiler_params=pltpu.CompilerParams(vmem_limit_bytes=limit * MB),
        cost_estimate=pl.CostEstimate(flops=flops, bytes_accessed=10**7, transcendentals=0),
    )


def after(x, *earlier):
    return lax.optimization_barrier((x,) + earlier)[0]


def to_chip(x, dx, dy):
    pairs = [
        (((a * 4 + b) * 2 + c), (((a + dx) % 2) * 4 + (b + dy) % 4) * 2 + c)
        for a in range(2)
        for b in range(4)
        for c in range(2)
    ]
    return lax.ppermute(x, "tensor", pairs)


def to_core(x):
    return lax.ppermute(x, "tensor", [(i, i ^ 1) for i in range(16)])


def pack_kernel(plan, n, *refs):
    for out, parts in zip(refs[n:], plan):
        row = 0
        for number, first, rows, turned in parts:
            value = refs[number][first : first + rows, :]
            value = value.T if turned else value
            out[row : row + value.shape[0], :] = value
            row += value.shape[0]


def pack(*outs, flops=10**6):
    arrays, index, plan, shapes = [], {}, [], []
    for parts in outs:
        steps, total, columns = [], 0, 0
        for array, *rows in parts:
            if id(array) not in index:
                index[id(array)] = len(arrays)
                arrays.append(array)
            first, count = rows or (0, array.shape[0])
            steps.append((index[id(array)], first, count, not rows))
            total += count if rows else array.shape[1]
            columns = array.shape[1] if rows else count
        plan.append(steps)
        shapes.append(struct((total, columns), BF16))
    made = call(
        functools.partial(pack_kernel, plan, len(arrays)),
        shapes,
        vmem(len(arrays)),
        vmem(len(shapes)),
        flops,
        12,
    )(*arrays)
    return made if len(made) > 1 else made[0]


def first_step(x):
    across, left, right = to_chip(x, 1, 0), to_chip(x, 0, 1), to_chip(x, 0, 3)
    return left, right, across


def second_step(left, right, across, to_right=(), to_left=(), flops=10**6):
    h = across.shape[0] // 2
    steps = pack(
        [(left, 0, h), (across, 0, h), *to_right],
        [(right, h, h), (across, h, h), *to_left],
        [(left, h, h), (right, 0, h)],
        flops=flops,
    )
    c, a, b = to_chip(steps[2], 1, 0), to_chip(steps[0], 0, 1), to_chip(steps[1], 0, 3)
    return steps, (a, b, c)


def most(x, left, right, across, a, b, c):
    rows = x.shape[0]
    own = pack([(array, 0, rows) for array in (x, left, right, across, a, b, c)])
    return own, to_core(own)


def most_plan(rows):
    h = rows // 2
    plan = []
    for other in range(2):
        for i, chip in enumerate((HERE, LEFT, RIGHT, ACROSS)):
            plan.append((other, i * rows, chip, 0, rows, other))
        for i, (chip, at) in enumerate(
            (
                (FAR, 0),
                (DIAG_LEFT, 0),
                (FAR, h),
                (DIAG_RIGHT, h),
                (DIAG_LEFT, h),
                (DIAG_RIGHT, 0),
            )
        ):
            plan.append((other, 4 * rows + i * h, chip, at, h, other))
    return plan


def last_plan(rows, joined):
    if joined:
        return [(other, 0, DIAG_FAR, 0, rows, other) for other in range(2)]
    h = rows // 2
    return [(2 * i + other, 0, DIAG_FAR, i * h, h, other) for i in range(2) for other in range(2)]


def shifted(plan, by):
    return [(number + by, *rest) for number, *rest in plan]


def chip_of(where, rel):
    return ((where[0] + rel[0]) % 2) * 4 + (where[1] + rel[1]) % 4


def assemble(plan, refs, full, where):
    share = full.shape[0] // 16
    for number, first, chip, at, n, other in plan:
        core = where[2] if other == 0 else 1 - where[2]
        row = pl.multiple_of((chip_of(where, chip) * 2 + core) * share + at, 32)
        full[pl.ds(row, n), :] = refs[number][first : first + n, :]


def clear(chip, full, where):
    wide = full.shape[0] // 8
    row = pl.multiple_of(chip_of(where, chip) * wide, 32)
    full[pl.ds(row, wide), :] = jnp.zeros((wide, full.shape[1]), full.dtype)


def far_rows(joined, refs, block, where):
    share = block.shape[0] // 2
    for number, first, chip, at, n, other in last_plan(share, joined):
        core = where[2] if other == 0 else 1 - where[2]
        row = pl.multiple_of(core * share + at, 32)
        block[pl.ds(row, n), :] = refs[number][first : first + n, :]
    return pl.ds(pl.multiple_of(chip_of(where, DIAG_FAR) * 2 * share, 128), 2 * share)


def start_assemble(plan, refs, full, where, sems):
    share = full.shape[0] // 16
    copies = []
    for i, (number, first, chip, at, n, other) in enumerate(plan):
        core = where[2] if other == 0 else 1 - where[2]
        row = pl.multiple_of((chip_of(where, chip) * 2 + core) * share + at, 32)
        copies.append(
            pltpu.make_async_copy(
                refs[number].at[pl.ds(first, n)], full.at[pl.ds(row, n)], sems.at[i]
            )
        )
    for copy in copies:
        copy.start()
    return copies


def fetch(pairs, sems, first=0):
    copies = [
        pltpu.make_async_copy(source, target, sems.at[first + i])
        for i, (source, target) in enumerate(pairs)
    ]
    for copy in copies:
        copy.start()
    return copies


def wait(copies):
    for copy in copies:
        copy.wait()


def route_kernel(ids_ref, gates_ref, grad_ref, routed_ref, pick_ref):
    top, tokens = ids_ref.shape
    slots = pick_ref.shape[0]
    groups = 16
    capacity = slots // groups
    expert = lax.broadcasted_iota(jnp.int32, (groups, tokens), 0)
    named = jnp.zeros((groups, tokens), F32)
    gate = jnp.zeros((groups, tokens), F32)
    for k in range(top):
        hit = expert == ids_ref[k : k + 1, :]
        named = named + jnp.where(hit, 1.0, 0.0)
        gate = gate + jnp.where(hit, gates_ref[k : k + 1, :], 0.0)
    earlier = lax.broadcasted_iota(jnp.int32, (tokens, tokens), 0) < lax.broadcasted_iota(
        jnp.int32, (tokens, tokens), 1
    )
    place = jnp.dot(
        named.astype(BF16),
        jnp.where(earlier, 1.0, 0.0).astype(BF16),
        preferred_element_type=F32,
    ).astype(jnp.int32)
    place = jnp.where(named > 0.5, place, -1)
    at = lax.broadcasted_iota(jnp.int32, (capacity, tokens), 0)
    half = capacity // 2
    for pair in range(0, groups, 2):
        rows, low, high = [], [], []
        for e in (pair, pair + 1):
            hit = at == place[e : e + 1, :]
            one = jnp.where(hit, 1.0, 0.0)
            scale = jnp.sum(jnp.where(hit, gate[e : e + 1, :], 0.0), axis=1, keepdims=True)
            picked = lax.dot_general(
                one.astype(BF16), grad_ref[...], NT, preferred_element_type=F32
            )
            rows.append(side_by_side(picked * scale, half))
            low.append(one[:half])
            high.append(one[half:])
        place_of = slice(pair * half, (pair + 2) * half)
        routed_ref[place_of, :] = jnp.concatenate(rows).astype(BF16)
        pick_ref[place_of, :] = jnp.concatenate(low).astype(BF16)
        pick_ref[groups * half + pair * half : groups * half + (pair + 2) * half, :] = (
            jnp.concatenate(high).astype(BF16)
        )


def side_by_side(rows, half):
    return jnp.concatenate([rows[:half], rows[half:]], axis=1)


def apart_kernel(routed_ref, out_ref):
    count, wide = routed_ref.shape
    share, capacity = wide // 2, 2 * count // 16
    rows = routed_ref[...].astype(F32).reshape(16, capacity // 2, wide)
    rows = jnp.concatenate([rows[:, :, :share], rows[:, :, share:]], axis=1)
    out_ref[...] = rows.reshape(2 * count, share).T.astype(BF16)


def sum_kernel(*refs):
    total = refs[0][...].astype(F32)
    for ref in refs[1:-1]:
        total = total + ref[...].astype(F32)
    share, slots = total.shape
    half = slots // 32
    rows = total.T.reshape(16, 2 * half, share)
    rows = jnp.concatenate([rows[:, :half], rows[:, half:]], axis=2)
    refs[-1][...] = rows.reshape(16 * half, 2 * share).astype(BF16)


def merge_kernel(own_ref, other_ref, c_ref, b_ref, a_ref, right_ref, left_ref, across_ref):
    h = c_ref.shape[0] // 2
    low, high = slice(0, h), slice(h, 2 * h)
    for out_ref, i, rows, part_ref, part in (
        (right_ref, 1, low, c_ref, high),
        (right_ref, 1, high, b_ref, low),
        (left_ref, 2, low, a_ref, low),
        (left_ref, 2, high, c_ref, low),
        (across_ref, 3, low, a_ref, high),
        (across_ref, 3, high, b_ref, high),
    ):
        total = own_ref[i, rows, :].astype(F32) + other_ref[i, rows, :].astype(F32)
        out_ref[rows, :] = (total + part_ref[part, :].astype(F32)).astype(BF16)


def combine_kernel(back_ref, pick_ref, out_ref):
    count, share = back_ref.shape[0], out_ref.shape[0]
    first = lax.dot_general(
        back_ref[...], pick_ref[:count, :], TN, preferred_element_type=F32
    )
    second = lax.dot_general(
        back_ref[...], pick_ref[count:, :], TN, preferred_element_type=F32
    )
    out_ref[...] = (first[:share] + second[share:]).astype(BF16)


def most_kernel(plan, where, own_ref, other_ref, *refs):
    n = (len(refs) - 1) // 2
    weights, outs, full = refs[:n], refs[n : 2 * n], refs[2 * n]
    clear(DIAG_FAR, full, where)
    assemble(plan, (own_ref, other_ref), full, where)
    for weight_ref, out_ref in zip(weights, outs):
        out_ref[...] = jnp.dot(weight_ref[...], full[...], preferred_element_type=F32)


def forward_kernel(where, own_ref, other_ref, gate_ref, up_ref, gate_most, up_most, *refs):
    act_ref, slope_ref, hidden_ref, block = refs
    far = far_rows(True, (own_ref, other_ref), block, where)
    width = 256
    for j in range(block.shape[1] // width):
        cols = slice(j * width, (j + 1) * width)
        x = block[:, cols]
        gate = gate_most[:, cols] + jnp.dot(gate_ref[:, far], x, preferred_element_type=F32)
        up = up_most[:, cols] + jnp.dot(up_ref[:, far], x, preferred_element_type=F32)
        sig = jax.nn.sigmoid(gate)
        act = gate * sig
        act_ref[:, cols] = act
        slope_ref[:, cols] = up * (sig * (1.0 + gate * (1.0 - sig)))
        hidden_ref[:, cols] = (act * up).astype(BF16)


def slot_blocks(rels, where, gate_ref, up_ref, d_gate, d_up, own_ref, other_ref):
    share = own_ref.shape[1]
    first_core = where[2] == 0
    for i, rel in enumerate(rels):
        cols = pl.ds(pl.multiple_of(chip_of(where, rel) * 2 * share, 128), 2 * share)
        block = lax.dot_general(
            gate_ref[:, cols], d_gate, TN, preferred_element_type=F32
        ) + lax.dot_general(up_ref[:, cols], d_up, TN, preferred_element_type=F32)
        low, high = block[:share].astype(BF16), block[share:].astype(BF16)
        own_ref[i] = jnp.where(first_core, low, high)
        other_ref[i] = jnp.where(first_core, high, low)


def backward_kernel(rels, where, *refs):
    pieces = refs[:4]
    down_ref, gate_ref, up_ref, act_ref, slope_ref, most_ref = refs[4:10]
    d_gate_ref, d_up_ref, own_ref, other_ref, block = refs[10:]
    far = far_rows(False, pieces, block, where)
    width = 256
    for j in range(block.shape[1] // width):
        cols = slice(j * width, (j + 1) * width)
        d_hidden = most_ref[:, cols] + jnp.dot(
            down_ref[:, far], block[:, cols], preferred_element_type=F32
        )
        d_gate_ref[:, cols] = (d_hidden * slope_ref[:, cols]).astype(BF16)
        d_up_ref[:, cols] = (d_hidden * act_ref[:, cols]).astype(BF16)
    slot_blocks(
        rels, where, gate_ref, up_ref, d_gate_ref[...], d_up_ref[...], own_ref, other_ref
    )


def slot_kernel(rels, where, gate_ref, up_ref, d_gate_ref, d_up_ref, own_ref, other_ref):
    slot_blocks(
        rels, where, gate_ref, up_ref, d_gate_ref[...], d_up_ref[...], own_ref, other_ref
    )


def weight_kernel(plans, where, *refs):
    inputs, routed = refs[:4], refs[4:10]
    hidden_ref, d_gate_ref, d_up_ref = refs[10:13]
    outs = refs[13:16]
    full, full_routed, *kept, sems, rsems, osems = refs[16:]
    parts = start_assemble(plans[0], inputs, full, where, sems)
    width = 512
    blocks = full.shape[0] // width
    wait(parts)
    routed_parts = start_assemble(plans[1], routed, full_routed, where, rsems)
    sent = []
    for k, (rows_ref, source) in enumerate(
        ((d_gate_ref, full), (d_up_ref, full), (hidden_ref, full_routed))
    ):
        if k == 2:
            wait(routed_parts)
        for j in range(blocks):
            cols = slice(j * width, (j + 1) * width)
            kept[k][:, cols] = lax.dot_general(
                rows_ref[...], source[cols, :], NT, preferred_element_type=F32
            ).astype(BF16)
            part = pl.ds(j * width, width)
            sent += fetch(
                [(kept[k].at[:, part], outs[k].at[:, part])], osems, k * blocks + j
            )
    wait(sent)


def plus(*terms):
    total = terms[0].astype(F32)
    for term in terms[1:]:
        total = total + term.astype(F32)
    return total.astype(BF16)


def shards(out_grad, expert_ids, gate_values, saved_inputs, w_gate, w_up, w_down):
    tokens, share = out_grad.shape
    slots = saved_inputs.shape[1]
    units = w_gate.shape[2]
    width = w_gate.shape[1]
    wide = 2 * share
    me = lax.axis_index("tensor")
    where = jnp.stack([me // 8, (me // 2) % 4, me % 2]).astype(jnp.int32)
    smem = [pl.BlockSpec(memory_space=pltpu.SMEM)]
    dma = pltpu.SemaphoreType.DMA
    gate_t, up_t, down = w_gate[0].T, w_up[0].T, w_down[0]
    one_matmul = 2 * slots * units * width

    routed, pick = call(
        route_kernel,
        (struct((slots // 2, wide), BF16), struct((slots, tokens), BF16)),
        vmem(3),
        vmem(2),
        2 * slots * tokens * share,
        60,
    )(expert_ids.T, gate_values.T, out_grad.T)
    h = share // 2
    plan = most_plan(share)
    plans = [plan + shifted(last_plan(share, joined), 2) for joined in (True, False)]
    x = saved_inputs[0].T
    left, right, across = first_step(x)
    steps, (a, b, c) = second_step(left, right, across)
    routed = lax.all_to_all(routed, "expert", split_axis=0, concat_axis=0, tiled=True)
    own, other = most(x, left, right, across, a, b, c)
    (r,) = call(
        apart_kernel, [struct((share, slots), BF16)], vmem(1), vmem(1), 10**6, 8
    )(after(routed, *steps))
    left, right, across = first_step(r)
    steps, (a, b, c) = second_step(
        left, right, across, [(a, h, h)], [(b, h, h)], 20000000000
    )

    def most_call(weights, where, own, other):
        n = len(weights)
        return call(
            functools.partial(most_kernel, plan),
            [struct((units, slots), F32)] * n,
            smem + vmem(n + 2),
            vmem(n),
            n * one_matmul,
            24,
            [pltpu.VMEM((width, slots), BF16)],
        )(where, own, other, *weights)

    gate_most, up_most = most_call((gate_t, up_t), after(where, *steps), own, other)
    a, b, c = lax.optimization_barrier((a, b, c, gate_most))[:3]
    e, f, last = pack([(a, h, h)], [(b, h, h)], [(a, share, h), (b, share, h)])
    input_pieces = (own, other, last, to_core(last))
    act, slope, hidden = call(
        forward_kernel,
        (
            struct((units, slots), F32),
            struct((units, slots), F32),
            struct((units, slots), BF16),
        ),
        smem + vmem(6),
        vmem(3),
        one_matmul,
        24,
        [pltpu.VMEM((wide, slots), BF16)],
    )(after(where, e), *input_pieces[2:], gate_t, up_t, gate_most, up_most)
    e, f = to_chip(e, 0, 1), to_chip(f, 0, 3)
    e, f = lax.optimization_barrier((e, f, act))[:2]
    own, other = most(r, left, right, across, a, b, c)
    (d_hidden_most,) = most_call((down,), where, own, other)
    routed_pieces = (own, other, e, to_core(e), f, to_core(f))

    def pair(count):
        return [struct((count, share, slots), BF16)] * 2

    rels = [DIAG_FAR], [DIAG_RIGHT, DIAG_LEFT, FAR], [HERE, RIGHT, LEFT, ACROSS]
    d_gate, d_up, own_a, other_a = call(
        functools.partial(backward_kernel, rels[0]),
        [struct((units, slots), BF16)] * 2 + pair(1),
        smem + vmem(10),
        vmem(4),
        one_matmul,
        24,
        [pltpu.VMEM((wide, slots), BF16)],
    )(where, *routed_pieces[2:], down, gate_t, up_t, act, slope, d_hidden_most)

    def slot_call(k, where):
        return call(
            functools.partial(slot_kernel, rels[k]),
            pair(len(rels[k])),
            smem + vmem(4),
            vmem(2),
            one_matmul,
            16,
        )(where, gate_t, up_t, d_gate, d_up)

    other_a = to_core(other_a)
    own_b, other_b = slot_call(1, where)
    far = plus(after(own_a[0], other_b), other_a[0])
    to_left, to_right = to_chip(far[:h], 0, 3), to_chip(far[h:], 0, 1)
    other_b = to_core(after(other_b, far))
    own_c, other_c = slot_call(2, after(where, far, other_b))
    diag_right = jnp.concatenate(
        [plus(own_b[0, :h], other_b[0, :h]), plus(own_b[0, h:], other_b[0, h:], to_right)]
    )
    diag_left = jnp.concatenate(
        [plus(own_b[1, :h], other_b[1, :h], to_left), plus(own_b[1, h:], other_b[1, h:])]
    )
    far = plus(own_b[2], other_b[2])
    steps = lax.optimization_barrier(
        (
            jnp.concatenate([far[:h], diag_left[:h]]),
            jnp.concatenate([far[h:], diag_right[h:]]),
            jnp.concatenate([diag_left[h:], diag_right[:h]]),
            own_c,
        )
    )
    other_c = to_core(other_c)
    c, b, a = to_chip(steps[2], 1, 0), to_chip(steps[1], 0, 1), to_chip(steps[0], 0, 3)
    right, left, across = call(
        merge_kernel,
        [struct((share, slots), BF16)] * 3,
        vmem(5),
        vmem(3),
        10**6,
        16,
    )(own_c, other_c, c, b, a)
    grad_gate, grad_up, grad_down = call(
        functools.partial(weight_kernel, plans),
        [struct((units, width), BF16)] * 3,
        smem + anywhere(10) + vmem(3),
        anywhere(3),
        3 * one_matmul,
        60,
        [pltpu.VMEM((width, slots), BF16)] * 2
        + [pltpu.VMEM((units, width), BF16)] * 3
        + [dma((len(plans[0]),)), dma((len(plans[1]),)), dma((3 * width // 512,))],
    )(after(where, left, right, across), *input_pieces, *routed_pieces, hidden, d_gate, d_up)
    across, right, left = to_chip(across, 1, 0), to_chip(right, 0, 1), to_chip(left, 0, 3)
    (summed,) = call(
        sum_kernel, [struct((slots // 2, wide), BF16)], vmem(5), vmem(1), 10**6, 8
    )(own_c[0], other_c[0], across, right, left)
    back = lax.all_to_all(summed, "expert", split_axis=0, concat_axis=0, tiled=True)
    (in_grad,) = call(
        combine_kernel,
        [struct((share, tokens), BF16)],
        vmem(2),
        vmem(1),
        2 * slots * tokens * share,
        8,
    )(back, pick)
    return in_grad.T, grad_gate.T[None], grad_up.T[None], grad_down[None]


def solution(mesh):
    return jax.shard_map(
        shards,
        mesh=mesh,
        in_specs=(
            P("expert", "tensor"),
            P("expert", None),
            P("expert", None),
            P("expert", None, "tensor"),
            P("expert", None, "tensor"),
            P("expert", None, "tensor"),
            P("expert", "tensor", None),
        ),
        out_specs=(
            P("expert", "tensor"),
            P("expert", None, "tensor"),
            P("expert", None, "tensor"),
            P("expert", "tensor", None),
        ),
        check_vma=False,
    )
```
